512 devices in a mesh: clip: 8 (over x, core), bank: 64 (over y, z).
Axes of the slice: x: 4, y: 8, z: 8, core: 2. Of those that a mesh axis runs over, the one named last changes fastest.
Arguments:
- queries: bfloat16 [8, 256, 1536], P('clip', 'bank'), may hold values from -120 to 120
- keys: bfloat16 [8, 8192, 1536], P('clip', 'bank'), may hold values from -6 to 6
- values: bfloat16 [8, 8192, 1536], P('clip', 'bank'), may hold values from -6 to 6
- grad_out: bfloat16 [8, 256, 1536], P('clip', 'bank'), may hold values from -6 to 6
- null_key: bfloat16 [1536], replicated, may hold values from -4 to 4
- null_value: bfloat16 [1536], replicated, may hold values from -4 to 4
- bank_counts: int32 [8], P('clip'), may hold values from 128 to 8192, as said below
- block_slot: int32 [8, 64], P('clip', 'bank'), may hold values from 0 to 63, each once within a row
Outputs:
- grad_queries: bfloat16 [8, 256, 1536], P('clip', 'bank')
- grad_keys: bfloat16 [8, 8192, 1536], P('clip', 'bank')
- grad_values: bfloat16 [8, 8192, 1536], P('clip', 'bank')
- grad_null_key: float32 [1536], replicated
- grad_null_value: float32 [1536], replicated
The draws below stay inside these ranges and needn't reach their ends.
Inputs may be any that keep to these rules, and one draw needn't show every extreme that they name: `bank_counts`: a multiple of 128; exactly one group holds 8192 live tokens. `block_slot`: each row is a permutation of the device indices.
All inputs are finite; a program needn't handle non-finite values.
Results may differ from the reference program's by a relative error of at most 0.01155.
Values may be sent and summed in bfloat16 or wider, within the bound.
No kernel may reach another device: no remote copies, remote signals or barrier semaphores. Data moves between devices by JAX's collectives and lax.ppermute only.
A program may use at most 64 MiB of HBM per device.

```python
import jax
import jax.numpy as jnp
from jax import lax

HEADS = 12
HD = 128
QTOK = 256
BLK = 128
HW = 1536
CLIPS = 8
BANK = 8192
N_BANK = 64


def pair_base(key):
    query_key = jax.random.fold_in(key, 101)
    bank_key = jax.random.fold_in(key, 102)
    query_base = jnp.clip(jax.random.normal(query_key, (CLIPS, QTOK, HW), jnp.float32), -6.0, 6.0)
    bank_base = jnp.clip(jax.random.normal(bank_key, (CLIPS, BANK, HW), jnp.float32), -6.0, 6.0)
    return (query_base, bank_base)


def draw_keys(key, part):
    query_base, bank_base = pair_base(key)
    return bank_base.astype(jnp.bfloat16)


def draw_queries(key, part):
    query_base, bank_base = pair_base(key)
    return query_base.astype(jnp.bfloat16)


def draw_bank_counts(key, part):
    key = jax.random.fold_in(key, 7)
    first_key, second_key = jax.random.split(key)
    busiest = jax.random.randint(first_key, (), 0, CLIPS)
    others = jax.random.randint(second_key, (CLIPS,), 1, BANK // 256 + 1)
    units = jnp.where(jnp.arange(CLIPS) == busiest, BANK // 128, others)
    return (units * 128).astype(jnp.int32)


def steps_of(key, extent, shards, low, top_value):
    factor_of, own = 1.0, jax.random.fold_in(key, 6)
    for axis_at, shards_of in shards:
        heights = jnp.exp(jax.random.uniform(jax.random.fold_in(own, axis_at), (shards_of,), jnp.float32, low / len(shards), top_value / len(shards)))
        factor_of = factor_of * jnp.repeat(heights, extent[axis_at] // shards_of).reshape([-1 if axis == axis_at else 1 for axis in range(len(extent))])
    return factor_of


def scatter_about(rng, extent, deviation, reach, shards=(), kind=jnp.bfloat16):
    factor_of = steps_of(rng, extent, shards, -0.22, 0.18) if shards else 1.0
    result = jax.random.normal(rng, extent, jnp.float32) * deviation * factor_of
    return jnp.minimum(jnp.maximum(result, -reach), reach).astype(kind)


def setup_inputs(seed: int = 0) -> dict:
    streams_of = jax.random.split(jax.random.key(seed), 9)
    queries = draw_queries(jax.random.fold_in(streams_of[8], 71), 0)
    keys = draw_keys(jax.random.fold_in(streams_of[8], 71), 0)
    values = scatter_about(streams_of[2], (CLIPS, BANK, HW), 1.0, 6.0, ((0, 8), (1, 64)))
    grad_out = scatter_about(streams_of[3], (CLIPS, QTOK, HW), 1.0, 6.0, ((0, 8), (1, 64)))
    null_key = scatter_about(streams_of[4], (HW,), 1.0, 4.0)
    null_value = scatter_about(streams_of[5], (HW,), 1.0, 4.0)
    bank_counts = draw_bank_counts(jax.random.fold_in(streams_of[8], 71), 0)
    block_slot = jax.vmap(lambda own: jax.random.permutation(own, N_BANK))(jax.random.split(streams_of[7], CLIPS)).reshape((CLIPS, N_BANK)).astype(jnp.int32)
    return dict(queries=queries, keys=keys, values=values, grad_out=grad_out, null_key=null_key, null_value=null_value, bank_counts=bank_counts, block_slot=block_slot)


def head_terms(pieces, live_keys):
    q_head, do_head, k_head, v_head, nk_head, nv_head = pieces
    score_scale = HD ** -0.5
    live_float = live_keys.astype(jnp.float32)
    scores = jnp.dot(q_head, k_head.T, preferred_element_type=jnp.float32) * score_scale
    scores = jnp.where(live_keys[None, :], scores, -1e30)
    null_score = jnp.dot(q_head, nk_head, preferred_element_type=jnp.float32) * score_scale
    row_top = jnp.maximum(jnp.max(scores, axis=1), null_score)
    totals = jnp.sum(jnp.exp(scores - row_top[:, None]) * live_float[None, :], axis=1) + jnp.exp(null_score - row_top)
    log_total = row_top + jnp.log(totals)
    probs = jnp.exp(scores - log_total[:, None]) * live_float[None, :]
    null_prob = jnp.exp(null_score - log_total)
    dprobs = jnp.dot(do_head, v_head.T, preferred_element_type=jnp.float32)
    null_dp = jnp.dot(do_head, nv_head, preferred_element_type=jnp.float32)
    row_delta = jnp.sum(probs * dprobs, axis=1) + null_prob * null_dp
    dscore = (probs * (dprobs - row_delta[:, None])).astype(jnp.bfloat16)
    null_ds = null_prob * (null_dp - row_delta)
    grad_q = (jnp.dot(dscore, k_head, preferred_element_type=jnp.float32) * score_scale
              + null_ds[:, None] * nk_head.astype(jnp.float32)[None, :] * score_scale).astype(jnp.bfloat16)
    grad_k = (jnp.dot(dscore.T, q_head, preferred_element_type=jnp.float32) * score_scale).astype(jnp.bfloat16)
    grad_v = jnp.dot(probs.astype(jnp.bfloat16).T, do_head, preferred_element_type=jnp.float32).astype(jnp.bfloat16)
    grad_nk = jnp.sum(null_ds[:, None] * q_head.astype(jnp.float32), axis=0) * score_scale
    grad_nv = jnp.sum(null_prob[:, None] * do_head.astype(jnp.float32), axis=0)
    return grad_q, grad_k, grad_v, grad_nk, grad_nv


def split_heads(matrix):
    return matrix.reshape(matrix.shape[0], HEADS, HD).transpose(1, 0, 2)


def join_heads(stacked):
    return stacked.transpose(1, 0, 2).reshape(stacked.shape[1], HEADS * HD)


def reference(queries, keys, values, grad_out, null_key, null_value, bank_counts, block_slot):
    nk_heads = null_key.reshape(HEADS, HD)
    nv_heads = null_value.reshape(HEADS, HD)

    def group_terms(pieces):
        q_group, k_group, v_group, do_group, count, slots = pieces
        positions = jnp.arange(BANK, dtype=jnp.int32)
        owner = positions // BLK
        logical = slots[owner] * BLK + positions % BLK
        live_keys = logical < count

        def one_head(items):
            return head_terms(items, live_keys)

        grad_q, grad_k, grad_v, grad_nk, grad_nv = lax.map(
            one_head, (split_heads(q_group), split_heads(do_group), split_heads(k_group), split_heads(v_group), nk_heads, nv_heads))
        return join_heads(grad_q), join_heads(grad_k), join_heads(grad_v), grad_nk.reshape(-1), grad_nv.reshape(-1)

    grad_q, grad_k, grad_v, grad_nk, grad_nv = lax.map(
        group_terms, (queries, keys, values, grad_out, bank_counts, block_slot))
    return grad_q, grad_k, grad_v, jnp.sum(grad_nk, axis=0), jnp.sum(grad_nv, axis=0)
```

```python
import functools

import jax
import jax.numpy as jnp
from jax import lax
from jax.experimental import pallas as pl
from jax.experimental.pallas import tpu as pltpu
from jax.sharding import Mesh, PartitionSpec as P

HEADS = 12
HD = 128
QTOK = 256
BLK = 128
HW = HEADS * HD
OWN = 4
PAD = 16
SCALE = HD ** (-0.5)
NT = (((1,), (1,)), ((), ()))
TN = (((0,), (0,)), ((), ()))


def dot(a, b, dims):
    return lax.dot_general(a, b, dims, preferred_element_type=jnp.float32)


def with_null(block, null_row):
    return jnp.concatenate([block, jnp.broadcast_to(null_row, (PAD, HD))], axis=0)


def stats_kernel(valid_ref, q_ref, do_ref, k_ref, v_ref, out_ref):
    live = lax.broadcasted_iota(jnp.int32, (BLK, QTOK), 0) < valid_ref[0]
    for h in range(HEADS):
        cols = slice(h * HD, (h + 1) * HD)
        scores = dot(k_ref[:, cols], q_ref[:, cols], NT) * SCALE
        scores = jnp.where(live, scores, -1e30)
        dprobs = dot(v_ref[:, cols], do_ref[:, cols], NT)
        top = jnp.max(scores, axis=0, keepdims=True)
        terms = jnp.where(live, jnp.exp(scores - top), 0.0)
        out_ref[0, h : h + 1, :] = top
        out_ref[1, h : h + 1, :] = jnp.sum(terms, axis=0, keepdims=True)
        out_ref[2, h : h + 1, :] = jnp.sum(terms * dprobs, axis=0, keepdims=True)


def merge_kernel(in_ref, out_ref):
    tops = in_ref[:, 0]
    top = jnp.max(tops, axis=0)
    weight = jnp.exp(tops - top[None])
    out_ref[0] = top
    out_ref[1] = jnp.sum(in_ref[:, 1] * weight, axis=0)
    out_ref[2] = jnp.sum(in_ref[:, 2] * weight, axis=0)


def grad_kernel(
    place_ref, parts_ref, q_ref, do_ref, k_ref, v_ref, nk_ref, nv_ref, dq_ref, dk_ref, dv_ref, null_ref
):
    live = lax.broadcasted_iota(jnp.int32, (BLK, QTOK), 0) < place_ref[0]
    first = place_ref[1] * OWN
    column = lax.broadcasted_iota(jnp.int32, (PAD, QTOK), 1)
    pad_row = lax.broadcasted_iota(jnp.int32, (PAD, QTOK), 0)
    own = (column >= first) & (column < first + OWN)
    tops = parts_ref[:, 0]
    bank_top = jnp.max(tops, axis=0)
    weight = jnp.exp(tops - bank_top[None])
    bank_sum = jnp.sum(parts_ref[:, 1] * weight, axis=0)
    bank_dot = jnp.sum(parts_ref[:, 2] * weight, axis=0)

    def hi_lo(row):
        hi = row.astype(jnp.bfloat16).astype(jnp.float32)
        return jnp.where(pad_row == 0, hi, jnp.where(pad_row == 1, row - hi, 0.0))

    for h in range(HEADS):
        cols = slice(h * HD, (h + 1) * HD)
        q, do = q_ref[:, cols], do_ref[:, cols]
        keys = with_null(k_ref[:, cols], nk_ref[:, cols])
        vals = with_null(v_ref[:, cols], nv_ref[:, cols])
        scores = dot(keys, q, NT) * SCALE
        dprobs = dot(vals, do, NT)
        null_score = scores[BLK : BLK + 1]
        null_dp = dprobs[BLK : BLK + 1]
        top = jnp.maximum(bank_top[h : h + 1], null_score)
        rest = jnp.exp(bank_top[h : h + 1] - top)
        null_term = jnp.exp(null_score - top)
        total = bank_sum[h : h + 1] * rest + null_term
        delta = (bank_dot[h : h + 1] * rest + null_term * null_dp) / total
        lse = top + jnp.log(total)
        probs = jnp.exp(jnp.where(live, scores[:BLK], -1e30) - lse)
        null_prob = jnp.exp(null_score - lse)
        dscore = (probs * (dprobs[:BLK] - delta)).astype(jnp.bfloat16)
        null_ds = hi_lo(null_prob * (null_dp - delta))
        null_pb = hi_lo(null_prob)
        wide_ds = jnp.concatenate([dscore, null_ds.astype(jnp.bfloat16)], axis=0)
        wide_pb = jnp.concatenate([probs.astype(jnp.bfloat16), null_pb.astype(jnp.bfloat16)], axis=0)
        own_ds = jnp.concatenate([dscore, jnp.where(own, null_ds, 0.0).astype(jnp.bfloat16)], axis=0)
        grad_k = jnp.dot(wide_ds, q, preferred_element_type=jnp.float32) * SCALE
        grad_v = jnp.dot(wide_pb, do, preferred_element_type=jnp.float32)
        dk_ref[:, cols] = grad_k[:BLK].astype(jnp.bfloat16)
        dv_ref[:, cols] = grad_v[:BLK].astype(jnp.bfloat16)
        null_ref[0:1, cols] = jnp.sum(grad_k[BLK:], axis=0, keepdims=True)
        null_ref[1:2, cols] = jnp.sum(grad_v[BLK:], axis=0, keepdims=True)
        dq_ref[:, cols] = (dot(own_ds, keys, TN) * SCALE).astype(jnp.bfloat16)


VMEM = pl.BlockSpec(memory_space=pltpu.VMEM)
SMEM = pl.BlockSpec(memory_space=pltpu.SMEM)
PARAMS = pltpu.CompilerParams(vmem_limit_bytes=32 * 1024 * 1024)


def spread(block, axes, count):
    return lax.all_to_all(jnp.broadcast_to(block[None], (count,) + block.shape), axes, 0, 0)


def on_device(queries, keys, values, grad_out, null_key, null_value, bank_counts, block_slot):
    bank = ("y", "z")
    valid = jnp.clip(bank_counts[0] - block_slot[0, 0] * BLK, 0, BLK)
    place = jnp.stack([valid, lax.axis_index(bank).astype(jnp.int32)])
    mine = jnp.concatenate([queries[0], grad_out[0]], axis=1)
    whole = spread(mine, bank, 64).reshape(QTOK, 2 * HW)
    whole_q, whole_do = whole[:, :HW], whole[:, HW:]
    parts = pl.pallas_call(
        stats_kernel,
        out_shape=jax.ShapeDtypeStruct((3, HEADS, QTOK), jnp.float32),
        in_specs=[SMEM, VMEM, VMEM, VMEM, VMEM],
        out_specs=VMEM,
        compiler_params=PARAMS,
        name="stats",
    )(place, whole_q, whole_do, keys[0], values[0])
    merged = pl.pallas_call(
        merge_kernel,
        out_shape=jax.ShapeDtypeStruct((3, HEADS, QTOK), jnp.float32),
        in_specs=[VMEM],
        out_specs=VMEM,
        compiler_params=PARAMS,
        name="merge",
    )(spread(parts, "z", 8))
    grad_q, grad_k, grad_v, nulls = pl.pallas_call(
        grad_kernel,
        out_shape=(
            jax.ShapeDtypeStruct((QTOK, HW), jnp.bfloat16),
            jax.ShapeDtypeStruct((BLK, HW), jnp.bfloat16),
            jax.ShapeDtypeStruct((BLK, HW), jnp.bfloat16),
            jax.ShapeDtypeStruct((2, HW), jnp.float32),
        ),
        in_specs=[SMEM] + [VMEM] * 7,
        out_specs=(VMEM,) * 4,
        compiler_params=PARAMS,
        name="grads",
    )(
        place,
        spread(merged, "y", 8),
        whole_q,
        whole_do,
        keys[0],
        values[0],
        null_key.reshape(1, HW),
        null_value.reshape(1, HW),
    )
    terms = lax.all_to_all(grad_q.reshape(64, OWN, HW), bank, 0, 0)
    own_q = jnp.sum(terms.astype(jnp.float32), axis=0).astype(jnp.bfloat16)
    null_sum = jnp.sum(spread(nulls, "clip", 8), axis=0)
    return (own_q[None], grad_k[None], grad_v[None], null_sum[0], null_sum[1])


def solution(mesh):
    grid = Mesh(mesh.devices.reshape(8, 8, 8), ("clip", "y", "z"))
    rows = P("clip", ("y", "z"), None)
    return jax.shard_map(
        on_device,
        mesh=grid,
        in_specs=(rows, rows, rows, rows, P(), P(), P("clip"), P("clip", ("y", "z"))),
        out_specs=(rows, rows, rows, P(), P()),
        check_vma=False,
    )
```

```python
import jax
import jax.numpy as jnp
from jax import lax
from jax.experimental import pallas as pl
from jax.experimental.pallas import tpu as pltpu
from jax.sharding import Mesh, PartitionSpec as P

HEADS = 12
HD = 128
QTOK = 256
BLK = 128
OWN = 4
QUAD = 4
MINE = HEADS // QUAD
WIDTH = MINE * HD
SLOTS = QUAD * BLK
PAD = 16
SCALE = HD ** (-0.5)
NT = (((1,), (1,)), ((), ()))
TN = (((0,), (0,)), ((), ()))
BANK = ("yq", "yb", "zq", "zb")
NEAR = ("yb", "zb")
FAR = ("yq", "zq")


def dot(a, b, dims):
    return lax.dot_general(a, b, dims, preferred_element_type=jnp.float32)


def columns_of(group):
    return pl.ds(pl.multiple_of(group * WIDTH, WIDTH), WIDTH)


def share_kernel(place_ref, k_ref, v_ref, *out_refs):
    live = jnp.broadcast_to((place_ref[0] > 0).astype(jnp.float32), (PAD, WIDTH)).astype(jnp.bfloat16)
    for hop, out_ref in enumerate(out_refs):
        cols = columns_of(place_ref[1] ^ hop)
        out_ref[:BLK] = k_ref[:, cols]
        out_ref[BLK : 2 * BLK] = v_ref[:, cols]
        out_ref[2 * BLK :] = live


def join_kernel(place_ref, *refs):
    for hop in range(QUAD):
        cols = columns_of(place_ref[1] ^ hop)
        refs[QUAD][:, cols] = refs[hop][:BLK]
        refs[QUAD + 1][:, cols] = refs[hop][BLK:]


def bank_scores(keys, q, blocks):
    scores = dot(keys, q, NT) * SCALE
    pieces = []
    for at, block in enumerate(blocks):
        live = block[2 * BLK :, :QTOK].astype(jnp.float32)[:1]
        bias = jnp.where(live > 0.5, 0.0, -1e30)
        pieces.append(scores[at * BLK : (at + 1) * BLK] + bias)
    return jnp.concatenate(pieces, axis=0), scores[SLOTS:]


def stats_kernel(qd_ref, b0, b1, b2, b3, out_ref):
    blocks = (b0, b1, b2, b3)
    for h in range(MINE):
        cols = slice(h * HD, (h + 1) * HD)
        q, do = qd_ref[:, cols], qd_ref[:, WIDTH + h * HD : WIDTH + (h + 1) * HD]
        keys = jnp.concatenate([b[:BLK, cols] for b in blocks], axis=0)
        vals = jnp.concatenate([b[BLK : 2 * BLK, cols] for b in blocks], axis=0)
        scores, _ = bank_scores(keys, q, blocks)
        dprobs = dot(vals, do, NT)
        top = jnp.max(scores, axis=0, keepdims=True)
        terms = jnp.exp(scores - top)
        rows = (top, jnp.sum(terms, axis=0, keepdims=True), jnp.sum(terms * dprobs, axis=0, keepdims=True))
        for at, row in enumerate(rows):
            out_ref[:, at, h : h + 1, :] = jnp.broadcast_to(row[None], (out_ref.shape[0], 1, QTOK))


def grad_kernel(place_ref, parts_ref, qd_ref, b0, b1, b2, b3, nk_ref, nv_ref, dq_ref, d0, d1, d2, d3, null_ref):
    blocks, outs = (b0, b1, b2, b3), (d0, d1, d2, d3)
    owner = lax.broadcasted_iota(jnp.int32, (PAD, QTOK), 1) // OWN
    pad_row = lax.broadcasted_iota(jnp.int32, (PAD, QTOK), 0)
    ours = ((owner >> 4) == place_ref[2]) & (((owner >> 1) & 3) == place_ref[3])
    tops = parts_ref[:, 0]
    bank_top = jnp.max(tops, axis=0)
    weight = jnp.exp(tops - bank_top[None])
    bank_sum = jnp.sum(parts_ref[:, 1] * weight, axis=0)
    bank_dot = jnp.sum(parts_ref[:, 2] * weight, axis=0)

    def hi_lo(row):
        hi = row.astype(jnp.bfloat16).astype(jnp.float32)
        return jnp.where(pad_row == 0, hi, jnp.where(pad_row == 1, row - hi, 0.0))

    def null_rows(ref, h):
        row = ref[:, columns_of(place_ref[1])][:, h * HD : (h + 1) * HD]
        return jnp.broadcast_to(row, (PAD, HD))

    for h in range(MINE):
        cols = slice(h * HD, (h + 1) * HD)
        q, do = qd_ref[:, cols], qd_ref[:, WIDTH + h * HD : WIDTH + (h + 1) * HD]
        keys = jnp.concatenate([b[:BLK, cols] for b in blocks] + [null_rows(nk_ref, h)], axis=0)
        vals = jnp.concatenate([b[BLK : 2 * BLK, cols] for b in blocks] + [null_rows(nv_ref, h)], axis=0)
        scores, null_scores = bank_scores(keys, q, blocks)
        dprobs = dot(vals, do, NT)
        null_score = null_scores[:1]
        null_dp = dprobs[SLOTS : SLOTS + 1]
        top = jnp.maximum(bank_top[h : h + 1], null_score)
        rest = jnp.exp(bank_top[h : h + 1] - top)
        null_term = jnp.exp(null_score - top)
        total = bank_sum[h : h + 1] * rest + null_term
        delta = (bank_dot[h : h + 1] * rest + null_term * null_dp) / total
        lse = top + jnp.log(total)
        probs = jnp.exp(scores - lse)
        null_prob = jnp.exp(null_score - lse)
        dscore = (probs * (dprobs[:SLOTS] - delta)).astype(jnp.bfloat16)
        null_ds = hi_lo(null_prob * (null_dp - delta))
        null_pb = hi_lo(null_prob)
        wide_ds = jnp.concatenate([dscore, null_ds.astype(jnp.bfloat16)], axis=0)
        wide_pb = jnp.concatenate([probs.astype(jnp.bfloat16), null_pb.astype(jnp.bfloat16)], axis=0)
        own_ds = jnp.concatenate([dscore, jnp.where(ours, null_ds, 0.0).astype(jnp.bfloat16)], axis=0)
        grad_k = jnp.dot(wide_ds, q, preferred_element_type=jnp.float32) * SCALE
        grad_v = jnp.dot(wide_pb, do, preferred_element_type=jnp.float32)
        for at, out in enumerate(outs):
            out[:BLK, cols] = grad_k[at * BLK : (at + 1) * BLK].astype(jnp.bfloat16)
            out[BLK:, cols] = grad_v[at * BLK : (at + 1) * BLK].astype(jnp.bfloat16)
        for at, grad in enumerate((grad_k, grad_v)):
            row = jnp.sum(grad[SLOTS:], axis=0, keepdims=True)
            null_ref[:, at : at + 1, cols] = jnp.broadcast_to(row[None], (null_ref.shape[0], 1, HD))
        dq_ref[:, cols] = (dot(own_ds, keys, TN) * SCALE).astype(jnp.bfloat16)


VMEM = pl.BlockSpec(memory_space=pltpu.VMEM)
SMEM = pl.BlockSpec(memory_space=pltpu.SMEM)


def kernel(body, name, ins, *outs):
    return pl.pallas_call(
        body,
        out_shape=tuple(jax.ShapeDtypeStruct(shape, dtype) for shape, dtype in outs),
        in_specs=ins,
        out_specs=(VMEM,) * len(outs),
        compiler_params=pltpu.CompilerParams(vmem_limit_bytes=32 * 1024 * 1024),
        name=name,
    )


def swap(blocks):
    return [blocks[0]] + [
        lax.ppermute(blocks[hop], NEAR, [(i, i ^ hop) for i in range(QUAD)]) for hop in range(1, QUAD)
    ]


def on_device(queries, keys, values, grad_out, null_key, null_value, bank_counts, block_slot):
    bf16, f32 = jnp.bfloat16, jnp.float32
    valid = jnp.clip(bank_counts[0] - block_slot[0, 0] * BLK, 0, BLK)
    place = jnp.stack(
        [valid] + [lax.axis_index(axes).astype(jnp.int32) for axes in (NEAR, "yq", "zq")]
    )
    pieces = jnp.stack([queries[0], grad_out[0]], axis=1).reshape(OWN, 2, 2, 2, WIDTH)
    pieces = pieces.transpose(2, 3, 0, 1, 4).reshape(1, 2, 1, 2, OWN, 2 * WIDTH)
    outgoing = jnp.broadcast_to(pieces, (4, 2, 4, 2, OWN, 2 * WIDTH)).reshape(64, OWN, 2 * WIDTH)
    whole = lax.all_to_all(outgoing, BANK, 0, 0).reshape(QTOK, 2 * WIDTH)
    blocks = swap(
        kernel(share_kernel, "share", [SMEM, VMEM, VMEM], *[((2 * BLK + PAD, WIDTH), bf16)] * QUAD)(
            place, keys[0], values[0]
        )
    )
    (parts,) = kernel(stats_kernel, "stats", [VMEM] * 5, ((16, 3, MINE, QTOK), f32))(whole, *blocks)
    parts = lax.all_to_all(parts, FAR, 0, 0)
    grad_q, *grad_kv, nulls = kernel(
        grad_kernel,
        "grads",
        [SMEM] + [VMEM] * 8,
        ((QTOK, WIDTH), bf16),
        *[((2 * BLK, WIDTH), bf16)] * QUAD,
        ((32, 2, WIDTH), f32),
    )(place, parts, whole, *blocks, null_key[None], null_value[None])
    terms = lax.all_to_all(grad_q.reshape(64, OWN, WIDTH), BANK, 0, 0).reshape(4, 2, 4, 2, OWN, WIDTH)
    own_q = jnp.sum(terms.astype(f32), axis=(0, 2)).astype(bf16).reshape(QUAD, OWN, WIDTH)
    own_q = own_q.transpose(1, 0, 2).reshape(1, OWN, HEADS * HD)
    grad_k, grad_v = kernel(
        join_kernel, "join", [SMEM] + [VMEM] * QUAD, *[((BLK, HEADS * HD), bf16)] * 2
    )(place, *swap(grad_kv))
    nulls = lax.all_to_all(nulls, ("clip",) + NEAR, 0, 0).reshape(8, QUAD, 2, WIDTH)
    nulls = jnp.sum(nulls, axis=0)
    return (own_q, grad_k[None], grad_v[None], nulls[:, 0].reshape(-1), nulls[:, 1].reshape(-1))


def solution(mesh):
    grid = Mesh(mesh.devices.reshape(8, 4, 2, 4, 2), ("clip",) + BANK)
    rows = P("clip", BANK, None)
    return jax.shard_map(
        on_device,
        mesh=grid,
        in_specs=(rows, rows, rows, rows, P(), P(), P("clip"), P("clip", BANK)),
        out_specs=(rows, rows, rows, P(), P()),
        check_vma=False,
    )
```

```python
import jax
import jax.numpy as jnp
from jax import lax
from jax.experimental import pallas as pl
from jax.experimental.pallas import tpu as pltpu
from jax.sharding import Mesh, PartitionSpec as P

HEADS = 12
HD = 128
QTOK = 256
BLK = 128
OWN = 4
QUAD = 4
MINE = HEADS // QUAD
WIDTH = MINE * HD
SLOTS = QUAD * BLK
PAD = 16
DEAD = 1024.0
SCALE = HD ** (-0.5)
NT = (((1,), (1,)), ((), ()))
TN = (((0,), (0,)), ((), ()))
BANK = ("yq", "yb", "zq", "zb")
NEAR = ("yb", "zb")
FAR = ("yq", "zq")


def dot(a, b, dims):
    return lax.dot_general(a, b, dims, preferred_element_type=jnp.float32)


def columns_of(group):
    return pl.ds(pl.multiple_of(group * WIDTH, WIDTH), WIDTH)


def outgoing_kernel(q_ref, do_ref, out_ref):
    for device in range(out_ref.shape[0]):
        group = ((device >> 3) & 1) * 2 + (device & 1)
        cols = slice(group * WIDTH, (group + 1) * WIDTH)
        out_ref[device, :, :WIDTH] = q_ref[:, cols]
        out_ref[device, :, WIDTH:] = do_ref[:, cols]


def share_kernel(place_ref, k_ref, v_ref, *out_refs):
    live = place_ref[0] > 0
    for hop, out_ref in enumerate(out_refs):
        cols = columns_of(place_ref[1] ^ hop)
        out_ref[:BLK] = jnp.where(live, k_ref[:, cols], jnp.bfloat16(DEAD))
        out_ref[BLK:] = v_ref[:, cols]


def join_kernel(place_ref, *refs):
    for hop in range(QUAD):
        cols = columns_of(place_ref[1] ^ hop)
        refs[QUAD][:, cols] = refs[hop][:BLK]
        refs[QUAD + 1][:, cols] = refs[hop][BLK:]


def bank_scores(keys, q, blocks):
    scores = dot(keys, q, NT) * SCALE
    pieces = []
    for at, block in enumerate(blocks):
        mark = block[:PAD, :QTOK].astype(jnp.float32)[:1]
        bias = jnp.where(mark < 0.5 * DEAD, 0.0, -1e30)
        pieces.append(scores[at * BLK : (at + 1) * BLK] + bias)
    return jnp.concatenate(pieces, axis=0), scores[SLOTS:]


def stats_kernel(qd_ref, b0, b1, b2, b3, out_ref):
    blocks = (b0, b1, b2, b3)
    for h in range(MINE):
        cols = slice(h * HD, (h + 1) * HD)
        q, do = qd_ref[:, cols], qd_ref[:, WIDTH + h * HD : WIDTH + (h + 1) * HD]
        keys = jnp.concatenate([b[:BLK, cols] for b in blocks], axis=0)
        vals = jnp.concatenate([b[BLK : 2 * BLK, cols] for b in blocks], axis=0)
        scores, _ = bank_scores(keys, q, blocks)
        dprobs = dot(vals, do, NT)
        top = jnp.max(scores, axis=0, keepdims=True)
        terms = jnp.exp(scores - top)
        rows = (top, jnp.sum(terms, axis=0, keepdims=True), jnp.sum(terms * dprobs, axis=0, keepdims=True))
        for at, row in enumerate(rows):
            out_ref[:, at, h : h + 1, :] = jnp.broadcast_to(row[None], (out_ref.shape[0], 1, QTOK))


def grad_kernel(place_ref, parts_ref, qd_ref, b0, b1, b2, b3, nk_ref, nv_ref, dq_ref, d0, d1, d2, d3):
    blocks, outs = (b0, b1, b2, b3), (d0, d1, d2, d3)
    owner = lax.broadcasted_iota(jnp.int32, (PAD, QTOK), 1) // OWN
    pad_row = lax.broadcasted_iota(jnp.int32, (PAD, QTOK), 0)
    ours = ((owner >> 4) == place_ref[2]) & (((owner >> 1) & 3) == place_ref[3])
    tops = parts_ref[:, 0]
    bank_top = jnp.max(tops, axis=0)
    weight = jnp.exp(tops - bank_top[None])
    bank_sum = jnp.sum(parts_ref[:, 1] * weight, axis=0)
    bank_dot = jnp.sum(parts_ref[:, 2] * weight, axis=0)

    def hi_lo(row):
        hi = row.astype(jnp.bfloat16).astype(jnp.float32)
        return jnp.where(pad_row == 0, hi, jnp.where(pad_row == 1, row - hi, 0.0))

    def null_rows(ref, h):
        row = ref[:, columns_of(place_ref[1])][:, h * HD : (h + 1) * HD]
        return jnp.broadcast_to(row, (PAD, HD))

    for h in range(MINE):
        cols = slice(h * HD, (h + 1) * HD)
        q, do = qd_ref[:, cols], qd_ref[:, WIDTH + h * HD : WIDTH + (h + 1) * HD]
        keys = jnp.concatenate([b[:BLK, cols] for b in blocks] + [null_rows(nk_ref, h)], axis=0)
        vals = jnp.concatenate([b[BLK : 2 * BLK, cols] for b in blocks] + [null_rows(nv_ref, h)], axis=0)
        scores, null_scores = bank_scores(keys, q, blocks)
        dprobs = dot(vals, do, NT)
        null_score = null_scores[:1]
        null_dp = dprobs[SLOTS : SLOTS + 1]
        top = jnp.maximum(bank_top[h : h + 1], null_score)
        rest = jnp.exp(bank_top[h : h + 1] - top)
        null_term = jnp.exp(null_score - top)
        total = bank_sum[h : h + 1] * rest + null_term
        delta = (bank_dot[h : h + 1] * rest + null_term * null_dp) / total
        lse = top + jnp.log(total)
        probs = jnp.exp(scores - lse)
        null_prob = jnp.exp(null_score - lse)
        dscore = (probs * (dprobs[:SLOTS] - delta)).astype(jnp.bfloat16)
        null_ds = hi_lo(null_prob * (null_dp - delta))
        null_pb = hi_lo(null_prob)
        wide_ds = jnp.concatenate([dscore, null_ds.astype(jnp.bfloat16)], axis=0)
        wide_pb = jnp.concatenate([probs.astype(jnp.bfloat16), null_pb.astype(jnp.bfloat16)], axis=0)
        own_ds = jnp.concatenate([dscore, jnp.where(ours, null_ds, 0.0).astype(jnp.bfloat16)], axis=0)
        grad_k = jnp.dot(wide_ds, q, preferred_element_type=jnp.float32) * SCALE
        grad_v = jnp.dot(wide_pb, do, preferred_element_type=jnp.float32)
        for at, out in enumerate(outs):
            out[:BLK, cols] = grad_k[at * BLK : (at + 1) * BLK].astype(jnp.bfloat16)
            out[BLK:, cols] = grad_v[at * BLK : (at + 1) * BLK].astype(jnp.bfloat16)
        null_grads = []
        for grad in (grad_k, grad_v):
            row = jnp.sum(grad[SLOTS:], axis=0, keepdims=True)
            hi = row.astype(jnp.bfloat16).astype(jnp.float32)
            null_grads += [hi, row - hi]
        null_grads = jnp.broadcast_to(jnp.concatenate(null_grads, axis=0)[None], (QTOK // OWN, 4, HD))
        grad_q = (dot(own_ds, keys, TN) * SCALE).reshape(QTOK // OWN, OWN, HD)
        dq_ref[:, :, cols] = jnp.concatenate([grad_q, null_grads], axis=1).astype(jnp.bfloat16)


def finish_kernel(terms_ref, q_ref, null_ref):
    for group in range(QUAD):
        cols = slice(group * WIDTH, (group + 1) * WIDTH)
        at = (group >> 1) * 8 + (group & 1)
        parts = terms_ref[at].astype(jnp.float32)
        total = parts
        for far in range(1, 16):
            total += terms_ref[at + (far >> 2) * 16 + (far & 3) * 2].astype(jnp.float32)
        q_ref[:, cols] = total[:OWN].astype(jnp.bfloat16)
        rows = jnp.concatenate([parts[4:5] + parts[5:6], parts[6:7] + parts[7:8]], axis=0)
        null_ref[:, :, cols] = jnp.broadcast_to(rows[None], (null_ref.shape[0], 2, WIDTH))


VMEM = pl.BlockSpec(memory_space=pltpu.VMEM)
SMEM = pl.BlockSpec(memory_space=pltpu.SMEM)


def kernel(body, name, ins, *outs):
    return pl.pallas_call(
        body,
        out_shape=tuple(jax.ShapeDtypeStruct(shape, dtype) for shape, dtype in outs),
        in_specs=ins,
        out_specs=(VMEM,) * len(outs),
        compiler_params=pltpu.CompilerParams(vmem_limit_bytes=32 * 1024 * 1024),
        name=name,
    )


def swap(blocks):
    return [blocks[0]] + [
        lax.ppermute(blocks[hop], NEAR, [(i, i ^ hop) for i in range(QUAD)]) for hop in range(1, QUAD)
    ]


def on_device(queries, keys, values, grad_out, null_key, null_value, bank_counts, block_slot):
    bf16, f32 = jnp.bfloat16, jnp.float32
    valid = jnp.clip(bank_counts[0] - block_slot[0, 0] * BLK, 0, BLK)
    place = jnp.stack(
        [valid] + [lax.axis_index(axes).astype(jnp.int32) for axes in (NEAR, "yq", "zq")]
    )
    (outgoing,) = kernel(outgoing_kernel, "outgoing", [VMEM] * 2, ((64, OWN, 2 * WIDTH), bf16))(
        queries[0], grad_out[0]
    )
    whole = lax.all_to_all(outgoing, BANK, 0, 0).reshape(QTOK, 2 * WIDTH)
    blocks = swap(
        kernel(share_kernel, "share", [SMEM, VMEM, VMEM], *[((2 * BLK, WIDTH), bf16)] * QUAD)(
            place, keys[0], values[0]
        )
    )
    (parts,) = kernel(stats_kernel, "stats", [VMEM] * 5, ((16, 3, MINE, QTOK), f32))(whole, *blocks)
    parts = lax.all_to_all(parts, FAR, 0, 0)
    grad_q, *grad_kv = kernel(
        grad_kernel,
        "grads",
        [SMEM] + [VMEM] * 8,
        ((64, 2 * OWN, WIDTH), bf16),
        *[((2 * BLK, WIDTH), bf16)] * QUAD,
    )(place, parts, whole, *blocks, null_key[None], null_value[None])
    terms = lax.all_to_all(grad_q, BANK, 0, 0)
    own_q, nulls = kernel(
        finish_kernel, "finish", [VMEM], ((OWN, HEADS * HD), bf16), ((8, 2, HEADS * HD), f32)
    )(terms)
    grad_k, grad_v = kernel(
        join_kernel, "join", [SMEM] + [VMEM] * QUAD, *[((BLK, HEADS * HD), bf16)] * 2
    )(place, *swap(grad_kv))
    nulls = jnp.sum(lax.all_to_all(nulls, "clip", 0, 0), axis=0)
    return (own_q[None], grad_k[None], grad_v[None], nulls[0], nulls[1])


def solution(mesh):
    grid = Mesh(mesh.devices.reshape(8, 4, 2, 4, 2), ("clip",) + BANK)
    rows = P("clip", BANK, None)
    return jax.shard_map(
        on_device,
        mesh=grid,
        in_specs=(rows, rows, rows, rows, P(), P(), P("clip"), P("clip", BANK)),
        out_specs=(rows, rows, rows, P(), P()),
        check_vma=False,
    )
```

```python
import jax
import jax.numpy as jnp
from jax import lax
from jax.experimental import pallas as pl
from jax.experimental.pallas import tpu as pltpu
from jax.sharding import Mesh, PartitionSpec as P

HEADS = 12
HD = 128
QTOK = 256
BLK = 128
OWN = 4
QUAD = 4
MINE = HEADS // QUAD
WIDTH = MINE * HD
SLOTS = QUAD * BLK
PAD = 16
DEAD = 1024.0
SCALE = HD ** (-0.5)
HOPS = (0, 3, 1, 2)
NT = (((1,), (1,)), ((), ()))
TN = (((0,), (0,)), ((), ()))
BANK = ("yq", "yb", "zq", "zb")
NEAR = ("yb", "zb")
FAR = ("yq", "zq")


def dot(a, b, dims):
    return lax.dot_general(a, b, dims, preferred_element_type=jnp.float32)


def columns_of(group):
    return pl.ds(pl.multiple_of(group * WIDTH, WIDTH), WIDTH)


def my_group():
    return lax.axis_index("yb") * 2 + lax.axis_index("zb")


def outgoing_kernel(q_hbm, do_hbm, out_ref, q_ref, do_ref, sems):
    copies = [
        pltpu.make_async_copy(q_hbm, q_ref, sems.at[0]),
        pltpu.make_async_copy(do_hbm, do_ref, sems.at[1]),
    ]
    for copy in copies:
        copy.start()
    for copy in copies:
        copy.wait()
    for device in range(out_ref.shape[0]):
        group = ((device >> 3) & 1) * 2 + (device & 1)
        cols = slice(group * WIDTH, (group + 1) * WIDTH)
        out_ref[device, :, :WIDTH] = q_ref[0, :, cols]
        out_ref[device, :, WIDTH:] = do_ref[0, :, cols]


def share_kernel(count_ref, slot_ref, k_ref, v_ref, *out_refs):
    live = count_ref[0] > slot_ref[0, 0] * BLK
    for hop, out_ref in zip(HOPS, out_refs):
        cols = columns_of(my_group() ^ hop)
        out_ref[:BLK] = jnp.where(live, k_ref[:, cols], jnp.bfloat16(DEAD))
        out_ref[BLK:] = v_ref[:, cols]


def join_kernel(*refs):
    for hop, block in zip(HOPS, refs):
        cols = columns_of(my_group() ^ hop)
        refs[QUAD][:, cols] = block[:BLK]
        refs[QUAD + 1][:, cols] = block[BLK:]


def bank_kernel(b0, b1, b2, b3, nk_ref, nv_ref, keys_ref, vals_ref):
    for at, block in enumerate((b0, b1, b2, b3)):
        keys_ref[at * BLK : (at + 1) * BLK] = block[:BLK]
        vals_ref[at * BLK : (at + 1) * BLK] = block[BLK:]
    for ref, out in ((nk_ref, keys_ref), (nv_ref, vals_ref)):
        out[SLOTS:] = jnp.broadcast_to(ref[:, columns_of(my_group())], (PAD, WIDTH))


def bank_scores(keys_ref, q, cols):
    scores = dot(keys_ref[:, cols], q, NT) * SCALE
    pieces = []
    for at in range(QUAD):
        mark = keys_ref[at * BLK : at * BLK + PAD, :QTOK].astype(jnp.float32)[:1]
        bias = jnp.where(mark < 0.5 * DEAD, 0.0, -1e30)
        pieces.append(scores[at * BLK : (at + 1) * BLK] + bias)
    return jnp.concatenate(pieces, axis=0), scores[SLOTS:]


def stats_kernel(qd_ref, keys_ref, vals_ref, out_ref):
    for h in range(MINE):
        cols = slice(h * HD, (h + 1) * HD)
        q, do = qd_ref[:, cols], qd_ref[:, WIDTH + h * HD : WIDTH + (h + 1) * HD]
        scores, _ = bank_scores(keys_ref, q, cols)
        dprobs = dot(vals_ref[:SLOTS, cols], do, NT)
        top = jnp.max(scores, axis=0, keepdims=True)
        terms = jnp.exp(scores - top)
        rows = (top, jnp.sum(terms, axis=0, keepdims=True), jnp.sum(terms * dprobs, axis=0, keepdims=True))
        for at, row in enumerate(rows):
            out_ref[:, at, h : h + 1, :] = jnp.broadcast_to(row[None], (out_ref.shape[0], 1, QTOK))


def grad_kernel(parts_ref, qd_ref, keys_ref, vals_ref, dq_ref, *outs):
    owner = lax.broadcasted_iota(jnp.int32, (PAD, QTOK), 1) // OWN
    pad_row = lax.broadcasted_iota(jnp.int32, (PAD, QTOK), 0)
    far_y, far_z = lax.axis_index("yq"), lax.axis_index("zq")
    ours = ((owner >> 4) == far_y) & (((owner >> 1) & 3) == far_z)
    carried = lax.rem(far_y * 4 + far_z, MINE)
    tops = parts_ref[:, 0]
    bank_top = jnp.max(tops, axis=0)
    weight = jnp.exp(tops - bank_top[None])
    bank_sum = jnp.sum(parts_ref[:, 1] * weight, axis=0)
    bank_dot = jnp.sum(parts_ref[:, 2] * weight, axis=0)

    def hi_lo(row):
        hi = row.astype(jnp.bfloat16).astype(jnp.float32)
        return jnp.where(pad_row == 0, hi, jnp.where(pad_row == 1, row - hi, 0.0))

    for h in range(MINE):
        cols = slice(h * HD, (h + 1) * HD)
        q, do = qd_ref[:, cols], qd_ref[:, WIDTH + h * HD : WIDTH + (h + 1) * HD]
        scores, null_scores = bank_scores(keys_ref, q, cols)
        dprobs = dot(vals_ref[:, cols], do, NT)
        null_score = null_scores[:1]
        null_dp = dprobs[SLOTS : SLOTS + 1]
        top = jnp.maximum(bank_top[h : h + 1], null_score)
        rest = jnp.exp(bank_top[h : h + 1] - top)
        null_term = jnp.exp(null_score - top)
        total = bank_sum[h : h + 1] * rest + null_term
        delta = (bank_dot[h : h + 1] * rest + null_term * null_dp) / total
        lse = top + jnp.log(total)
        probs = jnp.exp(scores - lse)
        null_prob = jnp.exp(null_score - lse)
        dscore = (probs * (dprobs[:SLOTS] - delta)).astype(jnp.bfloat16)
        null_ds = hi_lo(null_prob * (null_dp - delta))
        null_pb = hi_lo(null_prob)
        wide_ds = jnp.concatenate([dscore, null_ds.astype(jnp.bfloat16)], axis=0)
        wide_pb = jnp.concatenate([probs.astype(jnp.bfloat16), null_pb.astype(jnp.bfloat16)], axis=0)
        own_ds = jnp.concatenate([dscore, jnp.where(ours, null_ds, 0.0).astype(jnp.bfloat16)], axis=0)
        grad_k = jnp.dot(wide_ds, q, preferred_element_type=jnp.float32) * SCALE
        grad_v = jnp.dot(wide_pb, do, preferred_element_type=jnp.float32)
        for at, out in enumerate(outs):
            out[:BLK, cols] = grad_k[at * BLK : (at + 1) * BLK].astype(jnp.bfloat16)
            out[BLK:, cols] = grad_v[at * BLK : (at + 1) * BLK].astype(jnp.bfloat16)
        rows = []
        for grad in (grad_k, grad_v):
            row = jnp.sum(grad[SLOTS:], axis=0, keepdims=True)
            hi = row.astype(jnp.bfloat16).astype(jnp.float32)
            rows += [hi, row - hi]
        rows = jnp.concatenate(rows, axis=0)
        null_rows_out = rows if h == 0 else jnp.where(carried == h, rows, null_rows_out)
        grad_q = (dot(own_ds, keys_ref[:, cols], TN) * SCALE).reshape(QTOK // OWN, OWN, HD)
        dq_ref[:, :, cols] = grad_q.astype(jnp.bfloat16)
    dq_ref[:, :, WIDTH:] = jnp.broadcast_to(null_rows_out[None], (QTOK // OWN, OWN, HD)).astype(jnp.bfloat16)


def finish_kernel(terms_ref, q_ref, null_ref):
    def term(group, far):
        at = (group >> 1) * 8 + (group & 1) + (far >> 2) * 16 + (far & 3) * 2
        return terms_ref[at].astype(jnp.float32)

    for group in range(QUAD):
        total = term(group, 0)
        for far in range(1, 16):
            total += term(group, far)
        q_ref[:, group * WIDTH : (group + 1) * WIDTH] = total[:, :WIDTH].astype(jnp.bfloat16)
        for h in range(MINE):
            parts = term(group, h)[:, WIDTH:]
            rows = jnp.concatenate([parts[0:1] + parts[1:2], parts[2:3] + parts[3:4]], axis=0)
            at = group * WIDTH + h * HD
            null_ref[:, :, at : at + HD] = jnp.broadcast_to(rows[None], (null_ref.shape[0], 2, HD))


VMEM = pl.BlockSpec(memory_space=pltpu.VMEM)
SMEM = pl.BlockSpec(memory_space=pltpu.SMEM)


def kernel(body, name, ins, *outs, scratch=(), megabytes=32):
    return pl.pallas_call(
        body,
        out_shape=tuple(jax.ShapeDtypeStruct(shape, dtype) for shape, dtype in outs),
        in_specs=ins,
        out_specs=(VMEM,) * len(outs),
        scratch_shapes=scratch,
        compiler_params=pltpu.CompilerParams(vmem_limit_bytes=megabytes * 1024 * 1024),
        name=name,
    )


def partners(hop):
    pairs = []
    for clip in range(8):
        shift = clip & 1
        for y in range(8):
            for z in range(8):
                far_y = (((y + shift) ^ (hop >> 1)) - shift) % 8
                far_z = (((z + shift) ^ (hop & 1)) - shift) % 8
                pairs.append((clip * 64 + y * 8 + z, clip * 64 + far_y * 8 + far_z))
    return pairs


def swap(blocks):
    return [blocks[0]] + [
        lax.ppermute(block, ("clip",) + BANK, partners(hop)) for hop, block in zip(HOPS[1:], blocks[1:])
    ]


def on_device(queries, keys, values, grad_out, null_key, null_value, bank_counts, block_slot):
    bf16, f32 = jnp.bfloat16, jnp.float32
    (outgoing,) = kernel(
        outgoing_kernel,
        "outgoing",
        [pl.BlockSpec(memory_space=pltpu.HBM)] * 2,
        ((64, OWN, 2 * WIDTH), bf16),
        scratch=[pltpu.VMEM(queries.shape, bf16)] * 2 + [pltpu.SemaphoreType.DMA((2,))],
        megabytes=60,
    )(queries, grad_out)
    whole = lax.all_to_all(outgoing, BANK, 0, 0).reshape(QTOK, 2 * WIDTH)
    blocks = swap(
        kernel(share_kernel, "share", [SMEM, SMEM, VMEM, VMEM], *[((2 * BLK, WIDTH), bf16)] * QUAD)(
            bank_counts, block_slot, keys[0], values[0]
        )
    )
    keys, vals = kernel(
        bank_kernel,
        "bank",
        [VMEM] * 6,
        *[((SLOTS + PAD, WIDTH), bf16)] * 2,
    )(*blocks, null_key[None], null_value[None])
    (parts,) = kernel(stats_kernel, "stats", [VMEM] * 3, ((16, 3, MINE, QTOK), f32))(whole, keys, vals)
    parts = lax.all_to_all(parts, FAR, 0, 0)
    grad_q, *grad_kv = kernel(
        grad_kernel,
        "grads",
        [VMEM] * 4,
        ((64, OWN, WIDTH + HD), bf16),
        *[((2 * BLK, WIDTH), bf16)] * QUAD,
    )(parts, whole, keys, vals)
    terms = lax.all_to_all(grad_q, BANK, 0, 0)
    own_q, nulls = kernel(
        finish_kernel, "finish", [VMEM], ((OWN, HEADS * HD), bf16), ((8, 2, HEADS * HD), f32)
    )(terms)
    grad_k, grad_v = kernel(
        join_kernel, "join", [VMEM] * QUAD, *[((BLK, HEADS * HD), bf16)] * 2
    )(*swap(grad_kv))
    nulls = jnp.sum(lax.all_to_all(nulls, "clip", 0, 0), axis=0)
    return (own_q[None], grad_k[None], grad_v[None], nulls[0], nulls[1])


def solution(mesh):
    grid = Mesh(mesh.devices.reshape(8, 4, 2, 4, 2), ("clip",) + BANK)
    rows = P("clip", BANK, None)
    return jax.shard_map(
        on_device,
        mesh=grid,
        in_specs=(rows, rows, rows, rows, P(), P(), P("clip"), P("clip", BANK)),
        out_specs=(rows, rows, rows, P(), P()),
        check_vma=False,
    )
```

```python
import jax
import jax.numpy as jnp
from jax import lax
from jax.experimental import pallas as pl
from jax.experimental.pallas import tpu as pltpu
from jax.sharding import Mesh, PartitionSpec as P

HEADS = 12
HD = 128
QTOK = 256
BLK = 128
OWN = 4
QUAD = 4
MINE = HEADS // QUAD
WIDTH = MINE * HD
SLOTS = QUAD * BLK
PAD = 16
DEAD = 1024.0
SCALE = HD ** (-0.5)
HOPS = (0, 3, 1, 2)
NT = (((1,), (1,)), ((), ()))
TN = (((0,), (0,)), ((), ()))
BANK = ("yq", "yb", "zq", "zb")
NEAR = ("yb", "zb")
ALL = ("clip",) + BANK
GATHER_CORNER = (4, 0)
STATS_CORNER = (4, 4)
SUMS_CORNER = (0, 4)


def dot(a, b, dims):
    return lax.dot_general(a, b, dims, preferred_element_type=jnp.float32)


def columns_of(group):
    return pl.ds(pl.multiple_of(group * WIDTH, WIDTH), WIDTH)


def my_group():
    return lax.axis_index("yb") * 2 + lax.axis_index("zb")


def outgoing_kernel(q_hbm, do_hbm, out_ref, q_ref, do_ref, sems):
    copies = [
        pltpu.make_async_copy(q_hbm, q_ref, sems.at[0]),
        pltpu.make_async_copy(do_hbm, do_ref, sems.at[1]),
    ]
    for copy in copies:
        copy.start()
    for copy in copies:
        copy.wait()
    for device in range(out_ref.shape[0]):
        group = ((device >> 3) & 1) * 2 + (device & 1)
        cols = slice(group * WIDTH, (group + 1) * WIDTH)
        out_ref[device, :, :WIDTH] = q_ref[0, :, cols]
        out_ref[device, :, WIDTH:] = do_ref[0, :, cols]


def share_kernel(count_ref, slot_ref, k_ref, v_ref, *out_refs):
    live = count_ref[0] > slot_ref[0, 0] * BLK
    for hop, out_ref in zip(HOPS, out_refs):
        cols = columns_of(my_group() ^ hop)
        out_ref[:BLK] = jnp.where(live, k_ref[:, cols], jnp.bfloat16(DEAD))
        out_ref[BLK:] = v_ref[:, cols]


def join_kernel(*refs):
    for hop, block in zip(HOPS, refs):
        cols = columns_of(my_group() ^ hop)
        refs[QUAD][:, cols] = block[:BLK]
        refs[QUAD + 1][:, cols] = block[BLK:]


def bank_kernel(b0, b1, b2, b3, nk_ref, nv_ref, keys_ref, vals_ref):
    for at, block in enumerate((b0, b1, b2, b3)):
        keys_ref[at * BLK : (at + 1) * BLK] = block[:BLK]
        vals_ref[at * BLK : (at + 1) * BLK] = block[BLK:]
    for ref, out in ((nk_ref, keys_ref), (nv_ref, vals_ref)):
        out[SLOTS:] = jnp.broadcast_to(ref[:, columns_of(my_group())], (PAD, WIDTH))


def bank_scores(keys_ref, q, cols):
    scores = dot(keys_ref[:, cols], q, NT) * SCALE
    pieces = []
    for at in range(QUAD):
        mark = keys_ref[at * BLK : at * BLK + PAD, :QTOK].astype(jnp.float32)[:1]
        bias = jnp.where(mark < 0.5 * DEAD, 0.0, -1e30)
        pieces.append(scores[at * BLK : (at + 1) * BLK] + bias)
    return jnp.concatenate(pieces, axis=0), scores[SLOTS:]


def stats_kernel(qd_ref, keys_ref, vals_ref, out_ref):
    for h in range(MINE):
        cols = slice(h * HD, (h + 1) * HD)
        q, do = qd_ref[:, cols], qd_ref[:, WIDTH + h * HD : WIDTH + (h + 1) * HD]
        scores, _ = bank_scores(keys_ref, q, cols)
        dprobs = dot(vals_ref[:SLOTS, cols], do, NT)
        top = jnp.max(scores, axis=0, keepdims=True)
        terms = jnp.exp(scores - top)
        rows = (top, jnp.sum(terms, axis=0, keepdims=True), jnp.sum(terms * dprobs, axis=0, keepdims=True))
        for at, row in enumerate(rows):
            out_ref[:, at, h : h + 1, :] = jnp.broadcast_to(row[None], (out_ref.shape[0], 1, QTOK))


def grad_kernel(parts_ref, qd_ref, keys_ref, vals_ref, dq_ref, *outs):
    owner = lax.broadcasted_iota(jnp.int32, (PAD, QTOK), 1) // OWN
    pad_row = lax.broadcasted_iota(jnp.int32, (PAD, QTOK), 0)
    far_y, far_z = lax.axis_index("yq"), lax.axis_index("zq")
    owner_y = ((owner >> 4) + GATHER_CORNER[0] // 2) & 3
    owner_z = ((owner >> 1) + GATHER_CORNER[1] // 2) & 3
    ours = (owner_y == far_y) & (owner_z == far_z)
    far_at = ((far_y - SUMS_CORNER[0] // 2) & 3) * 4 + ((far_z - SUMS_CORNER[1] // 2) & 3)
    carried = lax.rem(far_at, MINE)
    tops = parts_ref[:, 0]
    bank_top = jnp.max(tops, axis=0)
    weight = jnp.exp(tops - bank_top[None])
    bank_sum = jnp.sum(parts_ref[:, 1] * weight, axis=0)
    bank_dot = jnp.sum(parts_ref[:, 2] * weight, axis=0)

    def hi_lo(row):
        hi = row.astype(jnp.bfloat16).astype(jnp.float32)
        return jnp.where(pad_row == 0, hi, jnp.where(pad_row == 1, row - hi, 0.0))

    for h in range(MINE):
        cols = slice(h * HD, (h + 1) * HD)
        q, do = qd_ref[:, cols], qd_ref[:, WIDTH + h * HD : WIDTH + (h + 1) * HD]
        scores, null_scores = bank_scores(keys_ref, q, cols)
        dprobs = dot(vals_ref[:, cols], do, NT)
        null_score = null_scores[:1]
        null_dp = dprobs[SLOTS : SLOTS + 1]
        top = jnp.maximum(bank_top[h : h + 1], null_score)
        rest = jnp.exp(bank_top[h : h + 1] - top)
        null_term = jnp.exp(null_score - top)
        total = bank_sum[h : h + 1] * rest + null_term
        delta = (bank_dot[h : h + 1] * rest + null_term * null_dp) / total
        lse = top + jnp.log(total)
        probs = jnp.exp(scores - lse)
        null_prob = jnp.exp(null_score - lse)
        dscore = (probs * (dprobs[:SLOTS] - delta)).astype(jnp.bfloat16)
        null_ds = hi_lo(null_prob * (null_dp - delta))
        null_pb = hi_lo(null_prob)
        wide_ds = jnp.concatenate([dscore, null_ds.astype(jnp.bfloat16)], axis=0)
        wide_pb = jnp.concatenate([probs.astype(jnp.bfloat16), null_pb.astype(jnp.bfloat16)], axis=0)
        own_ds = jnp.concatenate([dscore, jnp.where(ours, null_ds, 0.0).astype(jnp.bfloat16)], axis=0)
        grad_k = jnp.dot(wide_ds, q, preferred_element_type=jnp.float32) * SCALE
        grad_v = jnp.dot(wide_pb, do, preferred_element_type=jnp.float32)
        for at, out in enumerate(outs):
            out[:BLK, cols] = grad_k[at * BLK : (at + 1) * BLK].astype(jnp.bfloat16)
            out[BLK:, cols] = grad_v[at * BLK : (at + 1) * BLK].astype(jnp.bfloat16)
        rows = []
        for grad in (grad_k, grad_v):
            row = jnp.sum(grad[SLOTS:], axis=0, keepdims=True)
            hi = row.astype(jnp.bfloat16).astype(jnp.float32)
            rows += [hi, row - hi]
        rows = jnp.concatenate(rows, axis=0)
        null_rows_out = rows if h == 0 else jnp.where(carried == h, rows, null_rows_out)
        grad_q = (dot(own_ds, keys_ref[:, cols], TN) * SCALE).reshape(QTOK // OWN, OWN, HD)
        grad_q = grad_q.astype(jnp.bfloat16)
        for y in range(8):
            for z in range(0, 8, 4):
                at = (y + SUMS_CORNER[0] - GATHER_CORNER[0]) % 8 * 8 + (z + SUMS_CORNER[1] - GATHER_CORNER[1]) % 8
                dq_ref[y * 8 + z : y * 8 + z + 4, :, cols] = grad_q[at : at + 4]
    dq_ref[:, :, WIDTH:] = jnp.broadcast_to(null_rows_out[None], (QTOK // OWN, OWN, HD)).astype(jnp.bfloat16)


def term(terms_ref, group, far):
    at = (group >> 1) * 8 + (group & 1) + (far >> 2) * 16 + (far & 3) * 2
    return terms_ref[at].astype(jnp.float32)


def null_kernel(terms_ref, null_ref):
    for group in range(QUAD):
        for h in range(MINE):
            parts = term(terms_ref, group, h)[:, WIDTH:]
            rows = jnp.concatenate([parts[0:1] + parts[1:2], parts[2:3] + parts[3:4]], axis=0)
            at = group * WIDTH + h * HD
            null_ref[:, :, at : at + HD] = jnp.broadcast_to(rows[None], (null_ref.shape[0], 2, HD))


def own_kernel(terms_ref, q_ref):
    for group in range(QUAD):
        total = term(terms_ref, group, 0)
        for far in range(1, 16):
            total += term(terms_ref, group, far)
        q_ref[:, group * WIDTH : (group + 1) * WIDTH] = total[:, :WIDTH].astype(jnp.bfloat16)


def place(clip, y, z, corner):
    return clip * 64 + (y + corner[0]) % 8 * 8 + (z + corner[1]) % 8


def bank_groups(corner):
    return [[place(clip, y, z, corner) for y in range(8) for z in range(8)] for clip in range(8)]


def far_groups(corner):
    return [
        [place(clip, 2 * yq + yb, 2 * zq + zb, corner) for yq in range(4) for zq in range(4)]
        for clip in range(8)
        for yb in range(2)
        for zb in range(2)
    ]


VMEM = pl.BlockSpec(memory_space=pltpu.VMEM)
SMEM = pl.BlockSpec(memory_space=pltpu.SMEM)


def kernel(body, name, ins, *outs, scratch=(), megabytes=32):
    return pl.pallas_call(
        body,
        out_shape=tuple(jax.ShapeDtypeStruct(shape, dtype) for shape, dtype in outs),
        in_specs=ins,
        out_specs=(VMEM,) * len(outs),
        scratch_shapes=scratch,
        compiler_params=pltpu.CompilerParams(vmem_limit_bytes=megabytes * 1024 * 1024),
        name=name,
    )


def partners(hop):
    pairs = []
    for clip in range(8):
        shift = clip & 1
        for y in range(8):
            for z in range(8):
                far_y = (((y + shift) ^ (hop >> 1)) - shift) % 8
                far_z = (((z + shift) ^ (hop & 1)) - shift) % 8
                pairs.append((clip * 64 + y * 8 + z, clip * 64 + far_y * 8 + far_z))
    return pairs


def swap(blocks):
    return [blocks[0]] + [
        lax.ppermute(block, ("clip",) + BANK, partners(hop)) for hop, block in zip(HOPS[1:], blocks[1:])
    ]


def on_device(queries, keys, values, grad_out, null_key, null_value, bank_counts, block_slot):
    bf16, f32 = jnp.bfloat16, jnp.float32
    (outgoing,) = kernel(
        outgoing_kernel,
        "outgoing",
        [pl.BlockSpec(memory_space=pltpu.HBM)] * 2,
        ((64, OWN, 2 * WIDTH), bf16),
        scratch=[pltpu.VMEM(queries.shape, bf16)] * 2 + [pltpu.SemaphoreType.DMA((2,))],
        megabytes=60,
    )(queries, grad_out)
    whole = lax.all_to_all(outgoing, ALL, 0, 0, axis_index_groups=bank_groups(GATHER_CORNER), tiled=True)
    whole = whole.reshape(QTOK, 2 * WIDTH)
    blocks = swap(
        kernel(share_kernel, "share", [SMEM, SMEM, VMEM, VMEM], *[((2 * BLK, WIDTH), bf16)] * QUAD)(
            bank_counts, block_slot, keys[0], values[0]
        )
    )
    keys, vals = kernel(
        bank_kernel,
        "bank",
        [VMEM] * 6,
        *[((SLOTS + PAD, WIDTH), bf16)] * 2,
    )(*blocks, null_key[None], null_value[None])
    (parts,) = kernel(stats_kernel, "stats", [VMEM] * 3, ((16, 3, MINE, QTOK), f32))(whole, keys, vals)
    parts = lax.all_to_all(parts, ALL, 0, 0, axis_index_groups=far_groups(STATS_CORNER), tiled=True)
    grad_q, *grad_kv = kernel(
        grad_kernel,
        "grads",
        [VMEM] * 4,
        ((64, OWN, WIDTH + HD), bf16),
        *[((2 * BLK, WIDTH), bf16)] * QUAD,
    )(parts, whole, keys, vals)
    terms = lax.all_to_all(grad_q, ALL, 0, 0, axis_index_groups=bank_groups(SUMS_CORNER), tiled=True)
    (nulls,) = kernel(null_kernel, "nulls", [VMEM], ((8, 2, HEADS * HD), f32))(terms)
    (own_q,) = kernel(own_kernel, "own", [VMEM], ((OWN, HEADS * HD), bf16))(terms)
    grad_k, grad_v = kernel(
        join_kernel, "join", [VMEM] * QUAD, *[((BLK, HEADS * HD), bf16)] * 2
    )(*swap(grad_kv))
    nulls = jnp.sum(lax.all_to_all(nulls, "clip", 0, 0), axis=0)
    return (own_q[None], grad_k[None], grad_v[None], nulls[0], nulls[1])


def solution(mesh):
    grid = Mesh(mesh.devices.reshape(8, 4, 2, 4, 2), ("clip",) + BANK)
    rows = P("clip", BANK, None)
    return jax.shard_map(
        on_device,
        mesh=grid,
        in_specs=(rows, rows, rows, rows, P(), P(), P("clip"), P("clip", BANK)),
        out_specs=(rows, rows, rows, P(), P()),
        check_vma=False,
    )
```

```python
import jax
import jax.numpy as jnp
from jax import lax
from jax.experimental import pallas as pl
from jax.experimental.pallas import tpu as pltpu
from jax.sharding import Mesh, PartitionSpec as P

HEADS = 12
HD = 128
QTOK = 256
BLK = 128
OWN = 4
QUAD = 4
MINE = HEADS // QUAD
WIDTH = MINE * HD
SLOTS = QUAD * BLK
PAD = 16
DEAD = 1024.0
SCALE = HD ** (-0.5)
HOPS = (0, 3, 1, 2)
NT = (((1,), (1,)), ((), ()))
TN = (((0,), (0,)), ((), ()))
BANK = ("yq", "yb", "zq", "zb")
NEAR = ("yb", "zb")
ALL = ("clip",) + BANK
GATHER_CORNER = (4, 0)
STATS_CORNER = (2, 4)
SUMS_CORNER = (0, 4)


def dot(a, b, dims):
    return lax.dot_general(a, b, dims, preferred_element_type=jnp.float32)


def columns_of(group):
    return pl.ds(pl.multiple_of(group * WIDTH, WIDTH), WIDTH)


def my_group():
    return lax.axis_index("yb") * 2 + lax.axis_index("zb")


def outgoing_kernel(q_hbm, do_hbm, out_ref, q_ref, do_ref, sems):
    copies = [
        pltpu.make_async_copy(q_hbm, q_ref, sems.at[0]),
        pltpu.make_async_copy(do_hbm, do_ref, sems.at[1]),
    ]
    for copy in copies:
        copy.start()
    for copy in copies:
        copy.wait()
    for device in range(out_ref.shape[0]):
        group = ((device >> 3) & 1) * 2 + (device & 1)
        cols = slice(group * WIDTH, (group + 1) * WIDTH)
        out_ref[device, :, :WIDTH] = q_ref[0, :, cols]
        out_ref[device, :, WIDTH:] = do_ref[0, :, cols]


def share_kernel(count_ref, slot_ref, k_ref, v_ref, *out_refs):
    live = count_ref[0] > slot_ref[0, 0] * BLK
    for hop, out_ref in zip(HOPS, out_refs):
        cols = columns_of(my_group() ^ hop)
        out_ref[:BLK] = jnp.where(live, k_ref[:, cols], jnp.bfloat16(DEAD))
        out_ref[BLK:] = v_ref[:, cols]


def join_kernel(*refs):
    for hop, block in zip(HOPS, refs):
        cols = columns_of(my_group() ^ hop)
        refs[QUAD][:, cols] = block[:BLK]
        refs[QUAD + 1][:, cols] = block[BLK:]


def bank_kernel(b0, b1, b2, b3, nk_ref, nv_ref, keys_ref, vals_ref):
    for at, block in enumerate((b0, b1, b2, b3)):
        keys_ref[at * BLK : (at + 1) * BLK] = block[:BLK]
        vals_ref[at * BLK : (at + 1) * BLK] = block[BLK:]
    for ref, out in ((nk_ref, keys_ref), (nv_ref, vals_ref)):
        out[SLOTS:] = jnp.broadcast_to(ref[:, columns_of(my_group())], (PAD, WIDTH))


def bank_scores(keys_ref, q, cols):
    scores = dot(keys_ref[:, cols], q, NT) * SCALE
    pieces = []
    for at in range(QUAD):
        mark = keys_ref[at * BLK : at * BLK + PAD, :QTOK].astype(jnp.float32)[:1]
        bias = jnp.where(mark < 0.5 * DEAD, 0.0, -1e30)
        pieces.append(scores[at * BLK : (at + 1) * BLK] + bias)
    return jnp.concatenate(pieces, axis=0), scores[SLOTS:]


def stats_kernel(qd_ref, keys_ref, vals_ref, out_ref):
    for h in range(MINE):
        cols = slice(h * HD, (h + 1) * HD)
        q, do = qd_ref[:, cols], qd_ref[:, WIDTH + h * HD : WIDTH + (h + 1) * HD]
        scores, _ = bank_scores(keys_ref, q, cols)
        dprobs = dot(vals_ref[:SLOTS, cols], do, NT)
        top = jnp.max(scores, axis=0, keepdims=True)
        terms = jnp.exp(scores - top)
        rows = (top, jnp.sum(terms, axis=0, keepdims=True), jnp.sum(terms * dprobs, axis=0, keepdims=True))
        for at, row in enumerate(rows):
            out_ref[:, at, h : h + 1, :] = jnp.broadcast_to(row[None], (out_ref.shape[0], 1, QTOK))


def grad_kernel(parts_ref, qd_ref, keys_ref, vals_ref, dq_ref, *outs):
    owner = lax.broadcasted_iota(jnp.int32, (PAD, QTOK), 1) // OWN
    pad_row = lax.broadcasted_iota(jnp.int32, (PAD, QTOK), 0)
    far_y, far_z = lax.axis_index("yq"), lax.axis_index("zq")
    owner_y = ((owner >> 4) + GATHER_CORNER[0] // 2) & 3
    owner_z = ((owner >> 1) + GATHER_CORNER[1] // 2) & 3
    ours = (owner_y == far_y) & (owner_z == far_z)
    far_at = ((far_y - SUMS_CORNER[0] // 2) & 3) * 4 + ((far_z - SUMS_CORNER[1] // 2) & 3)
    carried = lax.rem(far_at, MINE)
    tops = parts_ref[:, 0]
    bank_top = jnp.max(tops, axis=0)
    weight = jnp.exp(tops - bank_top[None])
    bank_sum = jnp.sum(parts_ref[:, 1] * weight, axis=0)
    bank_dot = jnp.sum(parts_ref[:, 2] * weight, axis=0)

    def hi_lo(row):
        hi = row.astype(jnp.bfloat16).astype(jnp.float32)
        return jnp.where(pad_row == 0, hi, jnp.where(pad_row == 1, row - hi, 0.0))

    for h in range(MINE):
        cols = slice(h * HD, (h + 1) * HD)
        q, do = qd_ref[:, cols], qd_ref[:, WIDTH + h * HD : WIDTH + (h + 1) * HD]
        scores, null_scores = bank_scores(keys_ref, q, cols)
        dprobs = dot(vals_ref[:, cols], do, NT)
        null_score = null_scores[:1]
        null_dp = dprobs[SLOTS : SLOTS + 1]
        top = jnp.maximum(bank_top[h : h + 1], null_score)
        rest = jnp.exp(bank_top[h : h + 1] - top)
        null_term = jnp.exp(null_score - top)
        total = bank_sum[h : h + 1] * rest + null_term
        delta = (bank_dot[h : h + 1] * rest + null_term * null_dp) / total
        lse = top + jnp.log(total)
        probs = jnp.exp(scores - lse)
        null_prob = jnp.exp(null_score - lse)
        dscore = (probs * (dprobs[:SLOTS] - delta)).astype(jnp.bfloat16)
        null_ds = hi_lo(null_prob * (null_dp - delta))
        null_pb = hi_lo(null_prob)
        wide_ds = jnp.concatenate([dscore, null_ds.astype(jnp.bfloat16)], axis=0)
        wide_pb = jnp.concatenate([probs.astype(jnp.bfloat16), null_pb.astype(jnp.bfloat16)], axis=0)
        own_ds = jnp.concatenate([dscore, jnp.where(ours, null_ds, 0.0).astype(jnp.bfloat16)], axis=0)
        grad_k = jnp.dot(wide_ds, q, preferred_element_type=jnp.float32) * SCALE
        grad_v = jnp.dot(wide_pb, do, preferred_element_type=jnp.float32)
        for at, out in enumerate(outs):
            out[:BLK, cols] = grad_k[at * BLK : (at + 1) * BLK].astype(jnp.bfloat16)
            out[BLK:, cols] = grad_v[at * BLK : (at + 1) * BLK].astype(jnp.bfloat16)
        rows = []
        for grad in (grad_k, grad_v):
            row = jnp.sum(grad[SLOTS:], axis=0, keepdims=True)
            hi = row.astype(jnp.bfloat16).astype(jnp.float32)
            rows += [hi, row - hi]
        rows = jnp.concatenate(rows, axis=0)
        null_rows_out = rows if h == 0 else jnp.where(carried == h, rows, null_rows_out)
        grad_q = (dot(own_ds, keys_ref[:, cols], TN) * SCALE).reshape(QTOK // OWN, OWN, HD)
        grad_q = grad_q.astype(jnp.bfloat16)
        for y in range(8):
            for z in range(0, 8, 4):
                at = (y + SUMS_CORNER[0] - GATHER_CORNER[0]) % 8 * 8 + (z + SUMS_CORNER[1] - GATHER_CORNER[1]) % 8
                dq_ref[y * 8 + z : y * 8 + z + 4, :, cols] = grad_q[at : at + 4]
    dq_ref[:, :, WIDTH:] = jnp.broadcast_to(null_rows_out[None], (QTOK // OWN, OWN, HD)).astype(jnp.bfloat16)


def term(terms_ref, group, far):
    at = (group >> 1) * 8 + (group & 1) + (far >> 2) * 16 + (far & 3) * 2
    return terms_ref[at].astype(jnp.float32)


def null_kernel(terms_ref, null_ref):
    for group in range(QUAD):
        for h in range(MINE):
            parts = term(terms_ref, group, h)[:, WIDTH:]
            rows = jnp.concatenate([parts[0:1] + parts[1:2], parts[2:3] + parts[3:4]], axis=0)
            at = group * WIDTH + h * HD
            null_ref[:, :, at : at + HD] = jnp.broadcast_to(rows[None], (null_ref.shape[0], 2, HD))


def own_kernel(terms_ref, q_ref):
    for group in range(QUAD):
        total = term(terms_ref, group, 0)
        for far in range(1, 16):
            total += term(terms_ref, group, far)
        q_ref[:, group * WIDTH : (group + 1) * WIDTH] = total[:, :WIDTH].astype(jnp.bfloat16)


def place(clip, y, z, corner):
    return clip * 64 + (y + corner[0]) % 8 * 8 + (z + corner[1]) % 8


def bank_groups(corner):
    return [[place(clip, y, z, corner) for y in range(8) for z in range(8)] for clip in range(8)]


def far_groups(corner):
    return [
        [place(clip, 2 * yq + yb, 2 * zq + zb, corner) for yq in range(4) for zq in range(4)]
        for clip in range(8)
        for yb in range(2)
        for zb in range(2)
    ]


VMEM = pl.BlockSpec(memory_space=pltpu.VMEM)
SMEM = pl.BlockSpec(memory_space=pltpu.SMEM)


def kernel(body, name, ins, *outs, scratch=(), megabytes=32):
    return pl.pallas_call(
        body,
        out_shape=tuple(jax.ShapeDtypeStruct(shape, dtype) for shape, dtype in outs),
        in_specs=ins,
        out_specs=(VMEM,) * len(outs),
        scratch_shapes=scratch,
        compiler_params=pltpu.CompilerParams(vmem_limit_bytes=megabytes * 1024 * 1024),
        name=name,
    )


def partners(hop):
    pairs = []
    for clip in range(8):
        shift = clip & 1
        for y in range(8):
            for z in range(8):
                far_y = (((y + shift) ^ (hop >> 1)) - shift) % 8
                far_z = (((z + shift) ^ (hop & 1)) - shift) % 8
                pairs.append((clip * 64 + y * 8 + z, clip * 64 + far_y * 8 + far_z))
    return pairs


def swap(blocks):
    return [blocks[0]] + [
        lax.ppermute(block, ("clip",) + BANK, partners(hop)) for hop, block in zip(HOPS[1:], blocks[1:])
    ]


def on_device(queries, keys, values, grad_out, null_key, null_value, bank_counts, block_slot):
    bf16, f32 = jnp.bfloat16, jnp.float32
    (outgoing,) = kernel(
        outgoing_kernel,
        "outgoing",
        [pl.BlockSpec(memory_space=pltpu.HBM)] * 2,
        ((64, OWN, 2 * WIDTH), bf16),
        scratch=[pltpu.VMEM(queries.shape, bf16)] * 2 + [pltpu.SemaphoreType.DMA((2,))],
        megabytes=60,
    )(queries, grad_out)
    whole = lax.all_to_all(outgoing, ALL, 0, 0, axis_index_groups=bank_groups(GATHER_CORNER), tiled=True)
    whole = whole.reshape(QTOK, 2 * WIDTH)
    blocks = swap(
        kernel(share_kernel, "share", [SMEM, SMEM, VMEM, VMEM], *[((2 * BLK, WIDTH), bf16)] * QUAD)(
            bank_counts, block_slot, keys[0], values[0]
        )
    )
    keys, vals = kernel(
        bank_kernel,
        "bank",
        [VMEM] * 6,
        *[((SLOTS + PAD, WIDTH), bf16)] * 2,
    )(*blocks, null_key[None], null_value[None])
    (parts,) = kernel(stats_kernel, "stats", [VMEM] * 3, ((16, 3, MINE, QTOK), f32))(whole, keys, vals)
    parts = lax.all_to_all(parts, ALL, 0, 0, axis_index_groups=far_groups(STATS_CORNER), tiled=True)
    grad_q, *grad_kv = kernel(
        grad_kernel,
        "grads",
        [VMEM] * 4,
        ((64, OWN, WIDTH + HD), bf16),
        *[((2 * BLK, WIDTH), bf16)] * QUAD,
    )(parts, whole, keys, vals)
    terms = lax.all_to_all(grad_q, ALL, 0, 0, axis_index_groups=bank_groups(SUMS_CORNER), tiled=True)
    (nulls,) = kernel(null_kernel, "nulls", [VMEM], ((8, 2, HEADS * HD), f32))(terms)
    (own_q,) = kernel(own_kernel, "own", [VMEM], ((OWN, HEADS * HD), bf16))(terms)
    grad_k, grad_v = kernel(
        join_kernel, "join", [VMEM] * QUAD, *[((BLK, HEADS * HD), bf16)] * 2
    )(*swap(grad_kv))
    nulls = jnp.sum(lax.all_to_all(nulls, "clip", 0, 0), axis=0)
    return (own_q[None], grad_k[None], grad_v[None], nulls[0], nulls[1])


def solution(mesh):
    grid = Mesh(mesh.devices.reshape(8, 4, 2, 4, 2), ("clip",) + BANK)
    rows = P("clip", BANK, None)
    return jax.shard_map(
        on_device,
        mesh=grid,
        in_specs=(rows, rows, rows, rows, P(), P(), P("clip"), P("clip", BANK)),
        out_specs=(rows, rows, rows, P(), P()),
        check_vma=False,
    )
```

```python
import jax
import jax.numpy as jnp
from jax import lax
from jax.experimental import pallas as pl
from jax.experimental.pallas import tpu as pltpu
from jax.sharding import Mesh, PartitionSpec as P

HEADS = 12
HD = 128
QTOK = 256
BLK = 128
OWN = 4
QUAD = 4
MINE = HEADS // QUAD
WIDTH = MINE * HD
SLOTS = QUAD * BLK
PAD = 16
DEAD = 1024.0
SCALE = HD ** (-0.5)
HOPS = (0, 3, 1, 2)
NT = (((1,), (1,)), ((), ()))
TN = (((0,), (0,)), ((), ()))
BANK = ("yq", "yb", "zq", "zb")
NEAR = ("yb", "zb")
ALL = ("clip",) + BANK
GATHER_CORNER = (4, 0)
STATS_CORNER = (2, 4)
SUMS_CORNER = (0, 4)
CLIP_FIRST = 5


def dot(a, b, dims):
    return lax.dot_general(a, b, dims, preferred_element_type=jnp.float32)


def columns_of(group):
    return pl.ds(pl.multiple_of(group * WIDTH, WIDTH), WIDTH)


def my_group():
    return lax.axis_index("yb") * 2 + lax.axis_index("zb")


def outgoing_kernel(q_hbm, do_hbm, out_ref, q_ref, do_ref, sems):
    copies = [
        pltpu.make_async_copy(q_hbm, q_ref, sems.at[0]),
        pltpu.make_async_copy(do_hbm, do_ref, sems.at[1]),
    ]
    for copy in copies:
        copy.start()
    for copy in copies:
        copy.wait()
    for device in range(out_ref.shape[0]):
        group = ((device >> 3) & 1) * 2 + (device & 1)
        cols = slice(group * WIDTH, (group + 1) * WIDTH)
        out_ref[device, :, :WIDTH] = q_ref[0, :, cols]
        out_ref[device, :, WIDTH:] = do_ref[0, :, cols]


def share_kernel(count_ref, slot_ref, k_ref, v_ref, *out_refs):
    live = count_ref[0] > slot_ref[0, 0] * BLK
    for hop, out_ref in zip(HOPS, out_refs):
        cols = columns_of(my_group() ^ hop)
        out_ref[:BLK] = jnp.where(live, k_ref[:, cols], jnp.bfloat16(DEAD))
        out_ref[BLK:] = v_ref[:, cols]


def join_kernel(*refs):
    for hop, block in zip(HOPS, refs):
        cols = columns_of(my_group() ^ hop)
        refs[QUAD][:, cols] = block[:BLK]
        refs[QUAD + 1][:, cols] = block[BLK:]


def bank_kernel(b0, b1, b2, b3, nk_ref, nv_ref, keys_ref, vals_ref):
    for at, block in enumerate((b0, b1, b2, b3)):
        keys_ref[at * BLK : (at + 1) * BLK] = block[:BLK]
        vals_ref[at * BLK : (at + 1) * BLK] = block[BLK:]
    for ref, out in ((nk_ref, keys_ref), (nv_ref, vals_ref)):
        out[SLOTS:] = jnp.broadcast_to(ref[:, columns_of(my_group())], (PAD, WIDTH))


def bank_scores(keys_ref, q, cols):
    scores = dot(keys_ref[:, cols], q, NT) * SCALE
    pieces = []
    for at in range(QUAD):
        mark = keys_ref[at * BLK : at * BLK + PAD, :QTOK].astype(jnp.float32)[:1]
        bias = jnp.where(mark < 0.5 * DEAD, 0.0, -1e30)
        pieces.append(scores[at * BLK : (at + 1) * BLK] + bias)
    return jnp.concatenate(pieces, axis=0), scores[SLOTS:]


def stats_kernel(qd_ref, keys_ref, vals_ref, out_ref):
    for h in range(MINE):
        cols = slice(h * HD, (h + 1) * HD)
        q, do = qd_ref[:, cols], qd_ref[:, WIDTH + h * HD : WIDTH + (h + 1) * HD]
        scores, _ = bank_scores(keys_ref, q, cols)
        dprobs = dot(vals_ref[:SLOTS, cols], do, NT)
        top = jnp.max(scores, axis=0, keepdims=True)
        terms = jnp.exp(scores - top)
        rows = (top, jnp.sum(terms, axis=0, keepdims=True), jnp.sum(terms * dprobs, axis=0, keepdims=True))
        for at, row in enumerate(rows):
            out_ref[:, at, h : h + 1, :] = jnp.broadcast_to(row[None], (out_ref.shape[0], 1, QTOK))


def grad_kernel(parts_ref, qd_ref, keys_ref, vals_ref, dq_ref, *outs):
    owner = lax.broadcasted_iota(jnp.int32, (PAD, QTOK), 1) // OWN
    pad_row = lax.broadcasted_iota(jnp.int32, (PAD, QTOK), 0)
    far_y, far_z = lax.axis_index("yq"), lax.axis_index("zq")
    owner_y = ((owner >> 4) + GATHER_CORNER[0] // 2) & 3
    owner_z = ((owner >> 1) + GATHER_CORNER[1] // 2) & 3
    ours = (owner_y == far_y) & (owner_z == far_z)
    far_at = ((far_y - SUMS_CORNER[0] // 2) & 3) * 4 + ((far_z - SUMS_CORNER[1] // 2) & 3)
    carried = lax.rem(far_at, MINE)
    tops = parts_ref[:, 0]
    bank_top = jnp.max(tops, axis=0)
    weight = jnp.exp(tops - bank_top[None])
    bank_sum = jnp.sum(parts_ref[:, 1] * weight, axis=0)
    bank_dot = jnp.sum(parts_ref[:, 2] * weight, axis=0)

    def hi_lo(row):
        hi = row.astype(jnp.bfloat16).astype(jnp.float32)
        return jnp.where(pad_row == 0, hi, jnp.where(pad_row == 1, row - hi, 0.0))

    for h in range(MINE):
        cols = slice(h * HD, (h + 1) * HD)
        q, do = qd_ref[:, cols], qd_ref[:, WIDTH + h * HD : WIDTH + (h + 1) * HD]
        scores, null_scores = bank_scores(keys_ref, q, cols)
        dprobs = dot(vals_ref[:, cols], do, NT)
        null_score = null_scores[:1]
        null_dp = dprobs[SLOTS : SLOTS + 1]
        top = jnp.maximum(bank_top[h : h + 1], null_score)
        rest = jnp.exp(bank_top[h : h + 1] - top)
        null_term = jnp.exp(null_score - top)
        total = bank_sum[h : h + 1] * rest + null_term
        delta = (bank_dot[h : h + 1] * rest + null_term * null_dp) / total
        lse = top + jnp.log(total)
        probs = jnp.exp(scores - lse)
        null_prob = jnp.exp(null_score - lse)
        dscore = (probs * (dprobs[:SLOTS] - delta)).astype(jnp.bfloat16)
        null_ds = hi_lo(null_prob * (null_dp - delta))
        null_pb = hi_lo(null_prob)
        wide_ds = jnp.concatenate([dscore, null_ds.astype(jnp.bfloat16)], axis=0)
        wide_pb = jnp.concatenate([probs.astype(jnp.bfloat16), null_pb.astype(jnp.bfloat16)], axis=0)
        own_ds = jnp.concatenate([dscore, jnp.where(ours, null_ds, 0.0).astype(jnp.bfloat16)], axis=0)
        grad_k = jnp.dot(wide_ds, q, preferred_element_type=jnp.float32) * SCALE
        grad_v = jnp.dot(wide_pb, do, preferred_element_type=jnp.float32)
        for at, out in enumerate(outs):
            out[:BLK, cols] = grad_k[at * BLK : (at + 1) * BLK].astype(jnp.bfloat16)
            out[BLK:, cols] = grad_v[at * BLK : (at + 1) * BLK].astype(jnp.bfloat16)
        rows = []
        for grad in (grad_k, grad_v):
            row = jnp.sum(grad[SLOTS:], axis=0, keepdims=True)
            hi = row.astype(jnp.bfloat16).astype(jnp.float32)
            rows += [hi, row - hi]
        rows = jnp.concatenate(rows, axis=0)
        null_rows_out = rows if h == 0 else jnp.where(carried == h, rows, null_rows_out)
        grad_q = (dot(own_ds, keys_ref[:, cols], TN) * SCALE).reshape(QTOK // OWN, OWN, HD)
        grad_q = grad_q.astype(jnp.bfloat16)
        for y in range(8):
            for z in range(0, 8, 4):
                at = (y + SUMS_CORNER[0] - GATHER_CORNER[0]) % 8 * 8 + (z + SUMS_CORNER[1] - GATHER_CORNER[1]) % 8
                dq_ref[y * 8 + z : y * 8 + z + 4, :, cols] = grad_q[at : at + 4]
    dq_ref[:, :, WIDTH:] = jnp.broadcast_to(null_rows_out[None], (QTOK // OWN, OWN, HD)).astype(jnp.bfloat16)


def term(terms_ref, group, far):
    at = (group >> 1) * 8 + (group & 1) + (far >> 2) * 16 + (far & 3) * 2
    return terms_ref[at].astype(jnp.float32)


def null_kernel(terms_ref, null_ref):
    for group in range(QUAD):
        for h in range(MINE):
            parts = term(terms_ref, group, h)[:, WIDTH:]
            rows = jnp.concatenate([parts[0:1] + parts[1:2], parts[2:3] + parts[3:4]], axis=0)
            at = group * WIDTH + h * HD
            null_ref[:, :, at : at + HD] = jnp.broadcast_to(rows[None], (null_ref.shape[0], 2, HD))


def own_kernel(terms_ref, q_ref):
    for group in range(QUAD):
        total = term(terms_ref, group, 0)
        for far in range(1, 16):
            total += term(terms_ref, group, far)
        q_ref[:, group * WIDTH : (group + 1) * WIDTH] = total[:, :WIDTH].astype(jnp.bfloat16)


def place(clip, y, z, corner):
    return clip * 64 + (y + corner[0]) % 8 * 8 + (z + corner[1]) % 8


def bank_groups(corner):
    return [[place(clip, y, z, corner) for y in range(8) for z in range(8)] for clip in range(8)]


def clip_groups(first):
    return [[(clip + first) % 8 * 64 + at for clip in range(8)] for at in range(64)]


def far_groups(corner):
    return [
        [place(clip, 2 * yq + yb, 2 * zq + zb, corner) for yq in range(4) for zq in range(4)]
        for clip in range(8)
        for yb in range(2)
        for zb in range(2)
    ]


VMEM = pl.BlockSpec(memory_space=pltpu.VMEM)
SMEM = pl.BlockSpec(memory_space=pltpu.SMEM)


def kernel(body, name, ins, *outs, scratch=(), megabytes=32):
    return pl.pallas_call(
        body,
        out_shape=tuple(jax.ShapeDtypeStruct(shape, dtype) for shape, dtype in outs),
        in_specs=ins,
        out_specs=(VMEM,) * len(outs),
        scratch_shapes=scratch,
        compiler_params=pltpu.CompilerParams(vmem_limit_bytes=megabytes * 1024 * 1024),
        name=name,
    )


def partners(hop):
    pairs = []
    for clip in range(8):
        shift = clip & 1
        for y in range(8):
            for z in range(8):
                far_y = (((y + shift) ^ (hop >> 1)) - shift) % 8
                far_z = (((z + shift) ^ (hop & 1)) - shift) % 8
                pairs.append((clip * 64 + y * 8 + z, clip * 64 + far_y * 8 + far_z))
    return pairs


def swap(blocks):
    return [blocks[0]] + [
        lax.ppermute(block, ("clip",) + BANK, partners(hop)) for hop, block in zip(HOPS[1:], blocks[1:])
    ]


def on_device(queries, keys, values, grad_out, null_key, null_value, bank_counts, block_slot):
    bf16, f32 = jnp.bfloat16, jnp.float32
    (outgoing,) = kernel(
        outgoing_kernel,
        "outgoing",
        [pl.BlockSpec(memory_space=pltpu.HBM)] * 2,
        ((64, OWN, 2 * WIDTH), bf16),
        scratch=[pltpu.VMEM(queries.shape, bf16)] * 2 + [pltpu.SemaphoreType.DMA((2,))],
        megabytes=60,
    )(queries, grad_out)
    whole = lax.all_to_all(outgoing, ALL, 0, 0, axis_index_groups=bank_groups(GATHER_CORNER), tiled=True)
    whole = whole.reshape(QTOK, 2 * WIDTH)
    blocks = swap(
        kernel(share_kernel, "share", [SMEM, SMEM, VMEM, VMEM], *[((2 * BLK, WIDTH), bf16)] * QUAD)(
            bank_counts, block_slot, keys[0], values[0]
        )
    )
    keys, vals = kernel(
        bank_kernel,
        "bank",
        [VMEM] * 6,
        *[((SLOTS + PAD, WIDTH), bf16)] * 2,
    )(*blocks, null_key[None], null_value[None])
    (parts,) = kernel(stats_kernel, "stats", [VMEM] * 3, ((16, 3, MINE, QTOK), f32))(whole, keys, vals)
    parts = lax.all_to_all(parts, ALL, 0, 0, axis_index_groups=far_groups(STATS_CORNER), tiled=True)
    grad_q, *grad_kv = kernel(
        grad_kernel,
        "grads",
        [VMEM] * 4,
        ((64, OWN, WIDTH + HD), bf16),
        *[((2 * BLK, WIDTH), bf16)] * QUAD,
    )(parts, whole, keys, vals)
    terms = lax.all_to_all(grad_q, ALL, 0, 0, axis_index_groups=bank_groups(SUMS_CORNER), tiled=True)
    (nulls,) = kernel(null_kernel, "nulls", [VMEM], ((8, 2, HEADS * HD), f32))(terms)
    (own_q,) = kernel(own_kernel, "own", [VMEM], ((OWN, HEADS * HD), bf16))(terms)
    grad_k, grad_v = kernel(
        join_kernel, "join", [VMEM] * QUAD, *[((BLK, HEADS * HD), bf16)] * 2
    )(*swap(grad_kv))
    nulls = jnp.sum(lax.all_to_all(nulls, ALL, 0, 0, axis_index_groups=clip_groups(CLIP_FIRST), tiled=True), axis=0)
    return (own_q[None], grad_k[None], grad_v[None], nulls[0], nulls[1])


def solution(mesh):
    grid = Mesh(mesh.devices.reshape(8, 4, 2, 4, 2), ("clip",) + BANK)
    rows = P("clip", BANK, None)
    return jax.shard_map(
        on_device,
        mesh=grid,
        in_specs=(rows, rows, rows, rows, P(), P(), P("clip"), P("clip", BANK)),
        out_specs=(rows, rows, rows, P(), P()),
        check_vma=False,
    )
```

```python
import jax
import jax.numpy as jnp
from jax import lax
from jax.experimental import pallas as pl
from jax.experimental.pallas import tpu as pltpu
from jax.sharding import Mesh, PartitionSpec as P

HEADS = 12
HD = 128
QTOK = 256
BLK = 128
OWN = 4
QUAD = 4
MINE = HEADS // QUAD
WIDTH = MINE * HD
SLOTS = QUAD * BLK
PAD = 16
DEAD = 1024.0
SCALE = HD ** (-0.5)
HOPS = (0, 3, 1, 2)
NT = (((1,), (1,)), ((), ()))
TN = (((0,), (0,)), ((), ()))
BANK = ("yq", "yb", "zq", "zb")
NEAR = ("yb", "zb")
ALL = ("clip",) + BANK
GATHER_CORNER = (6, 0)
STATS_CORNER = (2, 4)
SUMS_CORNER = (0, 4)
CLIP_FIRST = 5


def dot(a, b, dims):
    return lax.dot_general(a, b, dims, preferred_element_type=jnp.float32)


def columns_of(group):
    return pl.ds(pl.multiple_of(group * WIDTH, WIDTH), WIDTH)


def my_group():
    return lax.axis_index("yb") * 2 + lax.axis_index("zb")


def outgoing_kernel(q_hbm, do_hbm, out_ref, q_ref, do_ref, sems):
    copies = [
        pltpu.make_async_copy(q_hbm, q_ref, sems.at[0]),
        pltpu.make_async_copy(do_hbm, do_ref, sems.at[1]),
    ]
    for copy in copies:
        copy.start()
    for copy in copies:
        copy.wait()
    for device in range(out_ref.shape[0]):
        group = ((device >> 3) & 1) * 2 + (device & 1)
        cols = slice(group * WIDTH, (group + 1) * WIDTH)
        out_ref[device, :, :WIDTH] = q_ref[0, :, cols]
        out_ref[device, :, WIDTH:] = do_ref[0, :, cols]


def share_kernel(count_ref, slot_ref, k_ref, v_ref, *out_refs):
    live = count_ref[0] > slot_ref[0, 0] * BLK
    for hop, out_ref in zip(HOPS, out_refs):
        cols = columns_of(my_group() ^ hop)
        out_ref[:BLK] = jnp.where(live, k_ref[:, cols], jnp.bfloat16(DEAD))
        out_ref[BLK:] = v_ref[:, cols]


def join_kernel(*refs):
    for hop, block in zip(HOPS, refs):
        cols = columns_of(my_group() ^ hop)
        refs[QUAD][:, cols] = block[:BLK]
        refs[QUAD + 1][:, cols] = block[BLK:]


def bank_kernel(b0, b1, b2, b3, nk_ref, nv_ref, keys_ref, vals_ref):
    for at, block in enumerate((b0, b1, b2, b3)):
        keys_ref[at * BLK : (at + 1) * BLK] = block[:BLK]
        vals_ref[at * BLK : (at + 1) * BLK] = block[BLK:]
    for ref, out in ((nk_ref, keys_ref), (nv_ref, vals_ref)):
        out[SLOTS:] = jnp.broadcast_to(ref[:, columns_of(my_group())], (PAD, WIDTH))


def bank_scores(keys_ref, q, cols):
    scores = dot(keys_ref[:, cols], q, NT) * SCALE
    pieces = []
    for at in range(QUAD):
        mark = keys_ref[at * BLK : at * BLK + PAD, :QTOK].astype(jnp.float32)[:1]
        bias = jnp.where(mark < 0.5 * DEAD, 0.0, -1e30)
        pieces.append(scores[at * BLK : (at + 1) * BLK] + bias)
    return jnp.concatenate(pieces, axis=0), scores[SLOTS:]


def stats_kernel(qd_ref, keys_ref, vals_ref, out_ref):
    for h in range(MINE):
        cols = slice(h * HD, (h + 1) * HD)
        q, do = qd_ref[:, cols], qd_ref[:, WIDTH + h * HD : WIDTH + (h + 1) * HD]
        scores, _ = bank_scores(keys_ref, q, cols)
        dprobs = dot(vals_ref[:SLOTS, cols], do, NT)
        top = jnp.max(scores, axis=0, keepdims=True)
        terms = jnp.exp(scores - top)
        rows = (top, jnp.sum(terms, axis=0, keepdims=True), jnp.sum(terms * dprobs, axis=0, keepdims=True))
        for at, row in enumerate(rows):
            out_ref[:, at, h : h + 1, :] = jnp.broadcast_to(row[None], (out_ref.shape[0], 1, QTOK))


def grad_kernel(parts_ref, qd_ref, keys_ref, vals_ref, dq_ref, *outs):
    owner = lax.broadcasted_iota(jnp.int32, (PAD, QTOK), 1) // OWN
    pad_row = lax.broadcasted_iota(jnp.int32, (PAD, QTOK), 0)
    far_y, far_z = lax.axis_index("yq"), lax.axis_index("zq")
    owner_y = ((owner >> 4) + GATHER_CORNER[0] // 2) & 3
    owner_z = ((owner >> 1) + GATHER_CORNER[1] // 2) & 3
    ours = (owner_y == far_y) & (owner_z == far_z)
    far_at = ((far_y - SUMS_CORNER[0] // 2) & 3) * 4 + ((far_z - SUMS_CORNER[1] // 2) & 3)
    carried = lax.rem(far_at, MINE)
    tops = parts_ref[:, 0]
    bank_top = jnp.max(tops, axis=0)
    weight = jnp.exp(tops - bank_top[None])
    bank_sum = jnp.sum(parts_ref[:, 1] * weight, axis=0)
    bank_dot = jnp.sum(parts_ref[:, 2] * weight, axis=0)

    def hi_lo(row):
        hi = row.astype(jnp.bfloat16).astype(jnp.float32)
        return jnp.where(pad_row == 0, hi, jnp.where(pad_row == 1, row - hi, 0.0))

    for h in range(MINE):
        cols = slice(h * HD, (h + 1) * HD)
        q, do = qd_ref[:, cols], qd_ref[:, WIDTH + h * HD : WIDTH + (h + 1) * HD]
        scores, null_scores = bank_scores(keys_ref, q, cols)
        dprobs = dot(vals_ref[:, cols], do, NT)
        null_score = null_scores[:1]
        null_dp = dprobs[SLOTS : SLOTS + 1]
        top = jnp.maximum(bank_top[h : h + 1], null_score)
        rest = jnp.exp(bank_top[h : h + 1] - top)
        null_term = jnp.exp(null_score - top)
        total = bank_sum[h : h + 1] * rest + null_term
        delta = (bank_dot[h : h + 1] * rest + null_term * null_dp) / total
        lse = top + jnp.log(total)
        probs = jnp.exp(scores - lse)
        null_prob = jnp.exp(null_score - lse)
        dscore = (probs * (dprobs[:SLOTS] - delta)).astype(jnp.bfloat16)
        null_ds = hi_lo(null_prob * (null_dp - delta))
        null_pb = hi_lo(null_prob)
        wide_ds = jnp.concatenate([dscore, null_ds.astype(jnp.bfloat16)], axis=0)
        wide_pb = jnp.concatenate([probs.astype(jnp.bfloat16), null_pb.astype(jnp.bfloat16)], axis=0)
        own_ds = jnp.concatenate([dscore, jnp.where(ours, null_ds, 0.0).astype(jnp.bfloat16)], axis=0)
        grad_k = jnp.dot(wide_ds, q, preferred_element_type=jnp.float32) * SCALE
        grad_v = jnp.dot(wide_pb, do, preferred_element_type=jnp.float32)
        for at, out in enumerate(outs):
            out[:BLK, cols] = grad_k[at * BLK : (at + 1) * BLK].astype(jnp.bfloat16)
            out[BLK:, cols] = grad_v[at * BLK : (at + 1) * BLK].astype(jnp.bfloat16)
        rows = []
        for grad in (grad_k, grad_v):
            row = jnp.sum(grad[SLOTS:], axis=0, keepdims=True)
            hi = row.astype(jnp.bfloat16).astype(jnp.float32)
            rows += [hi, row - hi]
        rows = jnp.concatenate(rows, axis=0)
        null_rows_out = rows if h == 0 else jnp.where(carried == h, rows, null_rows_out)
        grad_q = (dot(own_ds, keys_ref[:, cols], TN) * SCALE).reshape(QTOK // OWN, OWN, HD)
        grad_q = grad_q.astype(jnp.bfloat16)
        for y in range(8):
            for z in range(0, 8, 4):
                at = (y + SUMS_CORNER[0] - GATHER_CORNER[0]) % 8 * 8 + (z + SUMS_CORNER[1] - GATHER_CORNER[1]) % 8
                dq_ref[y * 8 + z : y * 8 + z + 4, :, cols] = grad_q[at : at + 4]
    dq_ref[:, :, WIDTH:] = jnp.broadcast_to(null_rows_out[None], (QTOK // OWN, OWN, HD)).astype(jnp.bfloat16)


def term(terms_ref, group, far):
    at = (group >> 1) * 8 + (group & 1) + (far >> 2) * 16 + (far & 3) * 2
    return terms_ref[at].astype(jnp.float32)


def null_kernel(terms_ref, null_ref):
    for group in range(QUAD):
        for h in range(MINE):
            parts = term(terms_ref, group, h)[:, WIDTH:]
            rows = jnp.concatenate([parts[0:1] + parts[1:2], parts[2:3] + parts[3:4]], axis=0)
            at = group * WIDTH + h * HD
            null_ref[:, :, at : at + HD] = jnp.broadcast_to(rows[None], (null_ref.shape[0], 2, HD))


def own_kernel(terms_ref, q_ref):
    for group in range(QUAD):
        total = term(terms_ref, group, 0)
        for far in range(1, 16):
            total += term(terms_ref, group, far)
        q_ref[:, group * WIDTH : (group + 1) * WIDTH] = total[:, :WIDTH].astype(jnp.bfloat16)


def place(clip, y, z, corner):
    return clip * 64 + (y + corner[0]) % 8 * 8 + (z + corner[1]) % 8


def bank_groups(corner):
    return [[place(clip, y, z, corner) for y in range(8) for z in range(8)] for clip in range(8)]


def clip_groups(first):
    return [[(clip + first) % 8 * 64 + at for clip in range(8)] for at in range(64)]


def far_groups(corner):
    return [
        [place(clip, 2 * yq + yb, 2 * zq + zb, corner) for yq in range(4) for zq in range(4)]
        for clip in range(8)
        for yb in range(2)
        for zb in range(2)
    ]


VMEM = pl.BlockSpec(memory_space=pltpu.VMEM)
SMEM = pl.BlockSpec(memory_space=pltpu.SMEM)


def kernel(body, name, ins, *outs, scratch=(), megabytes=32):
    return pl.pallas_call(
        body,
        out_shape=tuple(jax.ShapeDtypeStruct(shape, dtype) for shape, dtype in outs),
        in_specs=ins,
        out_specs=(VMEM,) * len(outs),
        scratch_shapes=scratch,
        compiler_params=pltpu.CompilerParams(vmem_limit_bytes=megabytes * 1024 * 1024),
        name=name,
    )


def partners(hop):
    pairs = []
    for clip in range(8):
        shift = clip & 1
        for y in range(8):
            for z in range(8):
                far_y = (((y + shift) ^ (hop >> 1)) - shift) % 8
                far_z = (((z + shift) ^ (hop & 1)) - shift) % 8
                pairs.append((clip * 64 + y * 8 + z, clip * 64 + far_y * 8 + far_z))
    return pairs


def swap(blocks):
    return [blocks[0]] + [
        lax.ppermute(block, ("clip",) + BANK, partners(hop)) for hop, block in zip(HOPS[1:], blocks[1:])
    ]


def on_device(queries, keys, values, grad_out, null_key, null_value, bank_counts, block_slot):
    bf16, f32 = jnp.bfloat16, jnp.float32
    (outgoing,) = kernel(
        outgoing_kernel,
        "outgoing",
        [pl.BlockSpec(memory_space=pltpu.HBM)] * 2,
        ((64, OWN, 2 * WIDTH), bf16),
        scratch=[pltpu.VMEM(queries.shape, bf16)] * 2 + [pltpu.SemaphoreType.DMA((2,))],
        megabytes=60,
    )(queries, grad_out)
    whole = lax.all_to_all(outgoing, ALL, 0, 0, axis_index_groups=bank_groups(GATHER_CORNER), tiled=True)
    whole = whole.reshape(QTOK, 2 * WIDTH)
    blocks = swap(
        kernel(share_kernel, "share", [SMEM, SMEM, VMEM, VMEM], *[((2 * BLK, WIDTH), bf16)] * QUAD)(
            bank_counts, block_slot, keys[0], values[0]
        )
    )
    keys, vals = kernel(
        bank_kernel,
        "bank",
        [VMEM] * 6,
        *[((SLOTS + PAD, WIDTH), bf16)] * 2,
    )(*blocks, null_key[None], null_value[None])
    (parts,) = kernel(stats_kernel, "stats", [VMEM] * 3, ((16, 3, MINE, QTOK), f32))(whole, keys, vals)
    parts = lax.all_to_all(parts, ALL, 0, 0, axis_index_groups=far_groups(STATS_CORNER), tiled=True)
    grad_q, *grad_kv = kernel(
        grad_kernel,
        "grads",
        [VMEM] * 4,
        ((64, OWN, WIDTH + HD), bf16),
        *[((2 * BLK, WIDTH), bf16)] * QUAD,
    )(parts, whole, keys, vals)
    terms = lax.all_to_all(grad_q, ALL, 0, 0, axis_index_groups=bank_groups(SUMS_CORNER), tiled=True)
    (nulls,) = kernel(null_kernel, "nulls", [VMEM], ((8, 2, HEADS * HD), f32))(terms)
    (own_q,) = kernel(own_kernel, "own", [VMEM], ((OWN, HEADS * HD), bf16))(terms)
    grad_k, grad_v = kernel(
        join_kernel, "join", [VMEM] * QUAD, *[((BLK, HEADS * HD), bf16)] * 2
    )(*swap(grad_kv))
    nulls = jnp.sum(lax.all_to_all(nulls, ALL, 0, 0, axis_index_groups=clip_groups(CLIP_FIRST), tiled=True), axis=0)
    return (own_q[None], grad_k[None], grad_v[None], nulls[0], nulls[1])


def solution(mesh):
    grid = Mesh(mesh.devices.reshape(8, 4, 2, 4, 2), ("clip",) + BANK)
    rows = P("clip", BANK, None)
    return jax.shard_map(
        on_device,
        mesh=grid,
        in_specs=(rows, rows, rows, rows, P(), P(), P("clip"), P("clip", BANK)),
        out_specs=(rows, rows, rows, P(), P()),
        check_vma=False,
    )
```
